32 devices in a mesh: ctx: 16 (over z, y, core), tp: 2 (over x).
Axes of the slice: x: 2, y: 2, z: 4, core: 2. Of those that a mesh axis runs over, the one named last changes fastest.
Arguments:
- tokens: bfloat16 [2, 1024, 896], P(None, 'ctx'), may hold values from -6 to 6
- cotangent: bfloat16 [2, 1024, 896], P(None, 'ctx'), may hold values from -6 to 6
- block_of: int32 [2, 32], replicated, may hold values from 0 to 31, as said below
- norm_gain: bfloat16 [896], P('ctx'), may hold values from 0.5 to 1.5
- ffn_gain: bfloat16 [896], P('ctx'), may hold values from 0.5 to 1.5
- w_query: bfloat16 [896, 896], P('ctx', 'tp'), may hold values from -0.1875 to 0.1875
- w_key: bfloat16 [896, 128], P('ctx', 'tp'), may hold values from -0.1875 to 0.1875
- w_value: bfloat16 [896, 128], P('ctx', 'tp'), may hold values from -0.1875 to 0.1875
- b_query: bfloat16 [896], P('tp'), may hold values from -3 to 3
- b_key: bfloat16 [128], P('tp'), may hold values from -3 to 3
- b_value: bfloat16 [128], P('tp'), may hold values from -3 to 3
- w_out: bfloat16 [896, 896], P('tp', 'ctx'), may hold values from -0.75 to 0.75
- w_gate: bfloat16 [896, 4864], P('ctx', 'tp'), may hold values from -0.1875 to 0.1875
- w_up: bfloat16 [896, 4864], P('ctx', 'tp'), may hold values from -0.1875 to 0.1875
- w_down: bfloat16 [4864, 896], P('tp', 'ctx'), may hold values from -0.078125 to 0.078125
Outputs:
- mixed: bfloat16 [2, 1024, 896], P(None, 'ctx')
- tokens_grad: bfloat16 [2, 1024, 896], P(None, 'ctx')
- norm_gain_grad: float32 [896], P('ctx')
- ffn_gain_grad: float32 [896], P('ctx')
- w_query_grad: float32 [896, 896], P('ctx', 'tp')
- w_key_grad: float32 [896, 128], P('ctx', 'tp')
- w_value_grad: float32 [896, 128], P('ctx', 'tp')
- b_query_grad: float32 [896], P('tp')
- b_key_grad: float32 [128], P('tp')
- b_value_grad: float32 [128], P('tp')
- w_out_grad: float32 [896, 896], P('tp', 'ctx')
- w_gate_grad: float32 [896, 4864], P('ctx', 'tp')
- w_up_grad: float32 [896, 4864], P('ctx', 'tp')
- w_down_grad: float32 [4864, 896], P('tp', 'ctx')
The draws below stay inside these ranges and needn't reach their ends.
Inputs may be any that keep to these rules, and one draw needn't show every extreme that they name: For each sequence s and each d < 16, entries 2d and 2d+1 of block_of[s] hold the blocks d and 31-d, in either order.
All inputs are finite; a program needn't handle non-finite values.
Results may differ from the reference program's by a relative error of at most 0.025.
Values may be sent and summed in bfloat16 or wider, within the bound.
No kernel may reach another device: no remote copies, remote signals or barrier semaphores. Data moves between devices by JAX's collectives and lax.ppermute only.
A program may use at most 192 MiB of HBM per device.

```python
import jax
import jax.numpy as jnp
from jax import lax

D = 896
HEADS = 14
KV_HEADS = 2
HEAD = 64
FF = 4864
SEQS = 2
BLK = 32
BLOCKS = 32
TOKENS = 1024


def draw_block_of(key, part):
    key = jax.random.fold_in(key, 11)
    halfway = BLOCKS // 2
    flips = jax.random.randint(key, (SEQS, halfway), 0, 2)
    lower = jnp.arange(halfway, dtype=jnp.int32)[None, :] + jnp.zeros((SEQS, 1), jnp.int32)
    upper = BLOCKS - 1 - lower
    first = jnp.where(flips == 1, upper, lower)
    second = jnp.where(flips == 1, lower, upper)
    return jnp.stack([first, second], axis=-1).reshape(SEQS, BLOCKS).astype(jnp.int32)


def spiked(entries, rng, source, target, parts, factor):
    owner, partner = [(jnp.arange(entries.shape[dim]) // (entries.shape[dim] // parts)).reshape([-1 if axis == dim else 1 for axis in range(entries.ndim)]) for dim in (source, target)]
    chosen = jax.random.permutation(rng, parts)[partner]
    strong = (owner == chosen) | (owner == (partner + parts // 2) % parts)
    return jnp.where(strong, factor * entries, entries)


def levels(key, extent, cuts, smallest, top_value):
    def one(position, blocks):
        steps = jax.random.uniform(jax.random.fold_in(jax.random.fold_in(key, 6), position), (blocks,), jnp.float32, smallest / len(cuts), top_value / len(cuts))
        return jnp.repeat(jnp.exp(steps), extent[position] // blocks).reshape((-1,) + (1,) * (len(extent) - position - 1))

    level = one(*cuts[0])
    for cut in cuts[1:]:
        level = level * one(*cut)
    return level


def noise(stream_key, extent, scale, bound, shards=(), held_as=jnp.bfloat16):
    values = scale * jax.random.normal(stream_key, extent, jnp.float32)
    if shards:
        values = values * levels(stream_key, extent, shards, -0.22, 0.18)
    return jnp.clip(values, -bound, bound).astype(held_as)


def heavy_noise(stream_key, dims, scale, limit, shards, heavy, kind=jnp.bfloat16):
    values = scale * jax.random.normal(stream_key, dims, jnp.float32)
    if shards:
        values = values * levels(stream_key, dims, shards, -0.22, 0.18)
    return jnp.clip(spiked(values, jax.random.fold_in(stream_key, 3), *heavy), -limit, limit).astype(kind)


def setup_inputs(seed: int = 0) -> dict:
    key_of = jax.random.split(jax.random.key(seed), 16)
    return {
        "tokens": noise(key_of[0], (SEQS, TOKENS, D), 1.0, 6.0, ((1, 16),)),
        "cotangent": heavy_noise(key_of[1], (SEQS, TOKENS, D), 1.0, 6.0, ((1, 16),), (1, 2, 16, 2.0)),
        "block_of": draw_block_of(jax.random.fold_in(key_of[15], 71), 0),
        "norm_gain": jnp.clip(1.0 + 0.1 * jax.random.normal(key_of[3], (D,), jnp.float32), 0.5, 1.5).astype(jnp.bfloat16),
        "ffn_gain": jnp.clip(1.0 + 0.1 * jax.random.normal(key_of[4], (D,), jnp.float32), 0.5, 1.5).astype(jnp.bfloat16),
        "w_query": noise(key_of[5], (D, HEADS * HEAD), D ** -0.5, 0.1875, ((0, 16), (1, 2))),
        "w_key": noise(key_of[6], (D, KV_HEADS * HEAD), D ** -0.5, 0.1875, ((0, 16), (1, 2))),
        "w_value": noise(key_of[7], (D, KV_HEADS * HEAD), D ** -0.5, 0.1875, ((0, 16), (1, 2))),
        "b_query": noise(key_of[8], (HEADS * HEAD,), 0.5, 3.0, ((0, 2),)),
        "b_key": noise(key_of[9], (KV_HEADS * HEAD,), 0.5, 3.0, ((0, 2),)),
        "b_value": noise(key_of[10], (KV_HEADS * HEAD,), 0.5, 3.0, ((0, 2),)),
        "w_out": noise(key_of[11], (HEADS * HEAD, D), (HEADS * HEAD // 16) ** -0.5, 0.75, ((0, 2), (1, 16))),
        "w_gate": noise(key_of[12], (D, FF), D ** -0.5, 0.1875, ((0, 16), (1, 2))),
        "w_up": noise(key_of[13], (D, FF), D ** -0.5, 0.1875, ((0, 16), (1, 2))),
        "w_down": noise(key_of[14], (FF, D), FF ** -0.5, 0.078125, ((0, 2), (1, 16))),
    }


EPSILON = 1e-06
ROPE_BASE = 1000000.0
HIGHEST = lax.Precision.HIGHEST

@jax.custom_vjp
def low(v):
    return lax.optimization_barrier(v.astype(jnp.bfloat16)).astype(jnp.float32)

@jax.custom_vjp
def low_back(v):
    return v

def low_keep(v):
    return (low(v), None)

def low_pass(kept, grad):
    return (grad,)

def back_keep(v):
    return (v, None)

def back_low(kept, grad):
    return (low(grad),)
low.defvjp(low_keep, low_pass)
low_back.defvjp(back_keep, back_low)

def rope_tables(positions, head_dim):
    halfway = head_dim // 2
    inverse = ROPE_BASE ** (-(jnp.arange(halfway, dtype=jnp.float32) * 2.0 / head_dim))
    angles = positions.astype(jnp.float32)[..., None] * inverse
    angles = jnp.concatenate([angles, angles], axis=-1)
    return (jnp.cos(angles), jnp.sin(angles))

def rotate(values, cosine, sine):
    halfway = values.shape[-1] // 2
    turned = jnp.concatenate([-values[..., halfway:], values[..., :halfway]], axis=-1)
    return values * cosine + turned * sine

def rms_norm(values, gain):
    return values * lax.rsqrt(lax.optimization_barrier(jnp.mean(values * values, axis=-1, keepdims=True)) + EPSILON) * gain

def project(values, matrix):
    return jnp.einsum('srd,df->srf', values, matrix, precision=HIGHEST)

def attend(queries, keys, values, positions):
    token_count = queries.shape[0]
    group = HEADS // KV_HEADS
    width = 512 if token_count % 512 == 0 else token_count
    keys_wide = jnp.repeat(keys, group, axis=1)
    values_wide = jnp.repeat(values, group, axis=1)
    factor = HEAD ** (-0.5)

    def one_block(inputs):
        query_block, query_pos = inputs
        scores = low_back(jnp.einsum('qhd,khd->hqk', query_block, keys_wide, precision=HIGHEST) * factor)
        allowed = positions[None, None, :] <= query_pos[None, :, None]
        highest = lax.optimization_barrier(jnp.max(jnp.where(allowed, scores, -1e+30), axis=-1, keepdims=True))
        raised = jnp.where(allowed, jnp.exp(scores - highest), 0.0)
        weights = low(raised / lax.optimization_barrier(jnp.sum(raised, axis=-1, keepdims=True)))
        return jnp.einsum('hqk,khd->qhd', weights, values_wide, precision=HIGHEST)
    blocks = token_count // width
    result = lax.map(jax.checkpoint(one_block), (queries.reshape(blocks, width, HEADS, HEAD), positions.reshape(blocks, width)))
    return result.reshape(token_count, HEADS, HEAD)

def layer(tokens, norm_gain, ffn_gain, w_query, w_key, w_value, b_query, b_key, b_value, w_out, w_gate, w_up, w_down, positions):
    seq_count, token_count, width = tokens.shape
    normed = low(rms_norm(tokens, norm_gain))
    query_lin = low_back(project(normed, w_query) + b_query)
    key_lin = low_back(project(normed, w_key) + b_key)
    value_lin = low(low_back(project(normed, w_value) + b_value))
    cosine, sine = rope_tables(positions, HEAD)
    cosine = cosine[:, :, None, :]
    sine = sine[:, :, None, :]
    queries = low(rotate(query_lin.reshape(seq_count, token_count, HEADS, HEAD), cosine, sine))
    keys = low(rotate(key_lin.reshape(seq_count, token_count, KV_HEADS, HEAD), cosine, sine))
    values = value_lin.reshape(seq_count, token_count, KV_HEADS, HEAD)
    outputs = jnp.stack([attend(queries[index], keys[index], values[index], positions[index]) for index in range(seq_count)])
    outputs = low(low_back(outputs.reshape(seq_count, token_count, HEADS * HEAD)))
    hidden = tokens + low_back(project(outputs, w_out))
    normed_two = low(rms_norm(hidden, ffn_gain))
    gate = low_back(project(normed_two, w_gate))
    up_values = low_back(project(normed_two, w_up))
    active = low(gate * jax.nn.sigmoid(gate) * up_values)
    return hidden + project(active, w_down)

def reference(tokens, cotangent, block_of, norm_gain, ffn_gain, w_query, w_key, w_value, b_query, b_key, b_value, w_out, w_gate, w_up, w_down):
    offsets = jnp.arange(BLK, dtype=jnp.int32)
    positions = (block_of.astype(jnp.int32)[:, :, None] * BLK + offsets).reshape(SEQS, TOKENS)
    inputs = [tokens, norm_gain, ffn_gain, w_query, w_key, w_value, b_query, b_key, b_value, w_out, w_gate, w_up, w_down]
    inputs = [item.astype(jnp.float32) for item in inputs]

    def forward(*items):
        return layer(*items, positions)
    result, pull = jax.vjp(forward, *inputs)
    grads = pull(cotangent.astype(jnp.float32))
    return (result.astype(jnp.bfloat16), grads[0].astype(jnp.bfloat16), grads[1], grads[2], grads[3], grads[4], grads[5], grads[6], grads[7], grads[8], grads[9], grads[10], grads[11], grads[12])
```

```python
import jax
import jax.numpy as jnp
from jax import lax
from jax.sharding import PartitionSpec as P

HEADS = 14
KV_HEADS = 2
HEAD = 64


EPSILON = 1e-06
ROPE_BASE = 1000000.0


def rope_tables(positions, head_dim):
    halfway = head_dim // 2
    inverse = ROPE_BASE ** (-(jnp.arange(halfway, dtype=jnp.float32) * 2.0 / head_dim))
    angles = positions.astype(jnp.float32)[..., None] * inverse
    angles = jnp.concatenate([angles, angles], axis=-1)
    return (jnp.cos(angles), jnp.sin(angles))


def rotate(values, cosine, sine):
    halfway = values.shape[-1] // 2
    turned = jnp.concatenate([-values[..., halfway:], values[..., :halfway]], axis=-1)
    return values * cosine + turned * sine


def unrotate(grads, cosine, sine):
    halfway = grads.shape[-1] // 2
    moved = grads * sine
    back = jnp.concatenate([moved[..., halfway:], -moved[..., :halfway]], axis=-1)
    return grads * cosine + back


def norm_apply(values, gain):
    factor = lax.rsqrt(jnp.mean(values * values, axis=-1, keepdims=True) + EPSILON)
    return (values * factor * gain, factor)


def norm_back(values, factor, gain, grads):
    weighted = grads * gain
    inner = jnp.mean(weighted * values, axis=-1, keepdims=True)
    d_values = factor * weighted - values * factor * factor * factor * inner
    d_gain = jnp.sum(grads * values * factor, axis=0)
    return (d_values, d_gain)


def dot(left, right, left_dim, right_dim):
    return lax.dot_general(
        left, right, (((left_dim,), (right_dim,)), ((), ())), preferred_element_type=jnp.float32
    )


class Groups:
    def __init__(self, count):
        self.count = count
        self.low = min(4, count)
        self.high = count // self.low
        self.near = [[h * self.low + k for k in range(self.low)] for h in range(self.high)]
        self.far = [[h * self.low + k for h in range(self.high)] for k in range(self.low)]

    def far_pairs(self, flip):
        return [(i, (i // self.low ^ flip) * self.low + i % self.low) for i in range(self.count)]

    def gather_near(self, values):
        return lax.all_gather(values, "ctx", axis=0, tiled=True, axis_index_groups=self.near)

    def gather_far(self, values):
        return lax.all_gather(values, "ctx", axis=0, tiled=True, axis_index_groups=self.far)

    def swap_near(self, values):
        return lax.all_to_all(values, "ctx", 0, 0, tiled=True, axis_index_groups=self.near)

    def from_far(self, values):
        return jnp.stack(
            [values]
            + [lax.ppermute(values, "ctx", self.far_pairs(m)) for m in range(1, self.high)]
        )

    def sum_far(self, pieces):
        total = pieces[0].astype(jnp.float32)
        for m in range(1, self.high):
            total = total + lax.ppermute(pieces[m], "ctx", self.far_pairs(m)).astype(jnp.float32)
        return total


def sum_tp(values):
    other = lax.ppermute(values, "tp", [(0, 1), (1, 0)])
    return values.astype(jnp.float32) + other.astype(jnp.float32)


def local(
    tokens,
    cotangent,
    block_of,
    norm_gain,
    ffn_gain,
    w_query,
    w_key,
    w_value,
    b_query,
    b_key,
    b_value,
    w_out,
    w_gate,
    w_up,
    w_down,
):
    seqs, rows, width = tokens.shape
    count = seqs * rows
    block_len = rows // 2
    ctx = lax.axis_size("ctx")
    groups = Groups(ctx)
    low, high = groups.low, groups.high
    device = lax.axis_index("ctx")
    factor = HEAD ** (-0.5)
    heads = w_query.shape[1] // HEAD
    share = width // ctx
    units = w_gate.shape[1]
    part = -(-units // (low * 128)) * 128

    gains = jnp.stack([norm_gain, ffn_gain], axis=1)
    w_attn = jnp.concatenate(
        [w_query, w_key, w_value, w_out.T, jnp.pad(gains, ((0, 0), (0, 126)))], axis=1
    )
    w_attn = lax.all_gather(w_attn, "ctx", axis=0, tiled=True)
    query_width = heads * HEAD
    qkv_width = query_width + 2 * HEAD
    w_qkv = w_attn[:, :qkv_width]
    w_out_t = w_attn[:, qkv_width : qkv_width + query_width]
    gains = w_attn[:, qkv_width + query_width : qkv_width + query_width + 2].astype(jnp.float32).T
    gain_one, gain_two = gains[0], gains[1]

    def pieces(matrix):
        return jnp.pad(matrix, ((0, 0), (0, low * part - units))).reshape(share, low, part)

    w_ffn = jnp.concatenate([pieces(w_gate), pieces(w_up), pieces(w_down.T)], axis=2)
    w_ffn = groups.swap_near(w_ffn.transpose(1, 0, 2)).reshape(low * share, 3 * part)
    w_ffn = groups.gather_far(w_ffn)
    w_gate_up, w_down_t = w_ffn[:, : 2 * part], w_ffn[:, 2 * part :]

    grads_in = cotangent.reshape(count, width)
    grads_near = groups.gather_near(grads_in)

    offsets = jnp.arange(block_len, dtype=jnp.int32)
    own_blocks = lax.dynamic_slice_in_dim(block_of, device * 2, 2, 1)
    row_pos = (own_blocks[:, :, None] * block_len + offsets).reshape(seqs, rows)
    owners = (device // low ^ jnp.arange(high, dtype=jnp.int32))[:, None] * low + jnp.arange(
        low, dtype=jnp.int32
    )
    key_blocks = block_of.reshape(seqs, ctx, 2)[:, owners.reshape(-1)]
    key_pos = (key_blocks[..., None] * block_len + offsets).reshape(seqs, ctx * rows)
    cosine, sine = rope_tables(row_pos.reshape(count), HEAD)
    cosine, sine = cosine[:, None, :], sine[:, None, :]

    inputs = tokens.astype(jnp.float32).reshape(count, width)
    normed, scale_one = norm_apply(inputs, gain_one)
    normed_low = normed.astype(jnp.bfloat16)
    bias = jnp.concatenate([b_query, b_key, b_value]).astype(jnp.float32)
    lin = dot(normed_low, w_qkv, 1, 0) + bias
    rotated = rotate(
        lin[:, : query_width + HEAD].reshape(count, heads + 1, HEAD), cosine, sine
    ).astype(jnp.bfloat16)
    queries = rotated[:, :heads].reshape(seqs, rows * heads, HEAD)
    query_pos = jnp.repeat(row_pos, heads, axis=1)
    pair = jnp.concatenate(
        [rotated[:, heads], lin[:, query_width + HEAD :].astype(jnp.bfloat16)], axis=1
    )
    near_pairs = groups.gather_near(pair)
    pairs = (
        groups.from_far(near_pairs)
        .reshape(high, low, seqs, rows, 2 * HEAD)
        .transpose(2, 0, 1, 3, 4)
        .reshape(seqs, ctx * rows, 2 * HEAD)
    )
    key_count = ctx * rows
    span = min(1024, key_count)

    def over_keys(step, state):
        if key_count == span:
            return step(state, pairs, key_pos)

        def inner(carry, index):
            some = lax.dynamic_slice_in_dim(pairs, index * span, span, 1)
            some_pos = lax.dynamic_slice_in_dim(key_pos, index * span, span, 1)
            return step(carry, some, some_pos)

        return lax.scan(inner, state, jnp.arange(key_count // span, dtype=jnp.int32))

    def block_scores(some, some_pos):
        scores = (
            jnp.einsum("aqd,akd->aqk", queries, some[..., :HEAD], preferred_element_type=jnp.float32)
            * factor
        )
        allowed = some_pos[:, None, :] <= query_pos[:, :, None]
        return scores, allowed

    def forward_step(state, some, some_pos):
        best, totals, summed = state
        scores, allowed = block_scores(some, some_pos)
        newest = jnp.maximum(best, jnp.max(jnp.where(allowed, scores, -1e30), axis=-1))
        raised = jnp.where(allowed, jnp.exp(scores - newest[..., None]), 0.0)
        fading = jnp.exp(best - newest)
        totals = totals * fading + jnp.sum(raised, axis=-1)
        summed = summed * fading[..., None] + jnp.einsum(
            "aqk,akd->aqd",
            raised.astype(jnp.bfloat16),
            some[..., HEAD:],
            preferred_element_type=jnp.float32,
        )
        return (newest, totals, summed), None

    state = (
        jnp.full((seqs, rows * heads), -1e30, jnp.float32),
        jnp.zeros((seqs, rows * heads), jnp.float32),
        jnp.zeros((seqs, rows * heads, HEAD), jnp.float32),
    )
    (best, totals, summed), _ = over_keys(forward_step, state)
    out_rows = summed / totals[..., None]
    log_total = best + jnp.log(totals)
    out_flat = out_rows.astype(jnp.bfloat16).reshape(count, query_width)
    attention = sum_tp(dot(out_flat, w_out_t, 1, 1).astype(jnp.bfloat16))
    hidden = inputs + attention

    normed_two, scale_two = norm_apply(hidden, gain_two)
    near_two = groups.gather_near(normed_two.astype(jnp.bfloat16))
    gate_up = dot(near_two, w_gate_up, 1, 0)
    gate, up_values = gate_up[:, :part], gate_up[:, part:]
    sigma = jax.nn.sigmoid(gate)
    active = (gate * sigma * up_values).astype(jnp.bfloat16)
    d_active = dot(grads_near, w_down_t, 1, 0)
    d_gate = (d_active * up_values * sigma * (1.0 + gate * (1.0 - sigma))).astype(jnp.bfloat16)
    d_up = (d_active * gate * sigma).astype(jnp.bfloat16)
    d_gate_up = jnp.concatenate([d_gate, d_up], axis=1)
    d_near = dot(d_gate_up, w_gate_up, 1, 1).astype(jnp.bfloat16)

    def home(values):
        swapped = groups.swap_near(values.reshape(low, count, width))
        return sum_tp(jnp.sum(swapped.astype(jnp.float32), axis=0).astype(jnp.bfloat16))

    d_normed_two = home(d_near)
    mixed = (hidden + home(dot(active, w_down_t, 1, 1).astype(jnp.bfloat16))).astype(jnp.bfloat16)
    d_w_ffn = jnp.concatenate(
        [dot(near_two, d_gate_up, 0, 0), dot(grads_near, active, 0, 0)], axis=1
    ).astype(jnp.bfloat16)
    d_w_ffn = lax.psum_scatter(
        d_w_ffn, "ctx", scatter_dimension=0, tiled=True, axis_index_groups=groups.far
    )
    d_w_ffn = groups.swap_near(d_w_ffn.reshape(low, share, 3 * part))
    d_w_ffn = d_w_ffn.transpose(1, 0, 2).astype(jnp.float32)

    def whole(index):
        some = d_w_ffn[:, :, index * part : (index + 1) * part]
        return some.reshape(share, low * part)[:, :units]

    g_gate, g_up, g_down = whole(0), whole(1), whole(2).T

    d_hidden_norm, d_gain_two = norm_back(hidden, scale_two, gain_two, d_normed_two)
    d_hidden = grads_in.astype(jnp.float32) + d_hidden_norm
    d_hidden_low = d_hidden.astype(jnp.bfloat16)
    d_out = dot(d_hidden_low, w_out_t, 1, 0).astype(jnp.bfloat16).reshape(seqs, rows * heads, HEAD)
    row_dots = jnp.sum(d_out.astype(jnp.float32) * out_rows, axis=-1)

    def backward_step(carry, some, some_pos):
        scores, allowed = block_scores(some, some_pos)
        chances = jnp.where(allowed, jnp.exp(scores - log_total[..., None]), 0.0)
        d_chances = jnp.einsum(
            "aqd,akd->aqk", d_out, some[..., HEAD:], preferred_element_type=jnp.float32
        )
        d_scores = (chances * (d_chances - row_dots[..., None])).astype(jnp.bfloat16)
        carry = (
            carry
            + jnp.einsum(
                "aqk,akd->aqd", d_scores, some[..., :HEAD], preferred_element_type=jnp.float32
            )
            * factor
        )
        d_keys = (
            jnp.einsum("aqk,aqd->akd", d_scores, queries, preferred_element_type=jnp.float32)
            * factor
        )
        d_values = jnp.einsum(
            "aqk,aqd->akd",
            chances.astype(jnp.bfloat16),
            d_out,
            preferred_element_type=jnp.float32,
        )
        return carry, jnp.concatenate([d_keys, d_values], axis=-1).astype(jnp.bfloat16)

    d_query, d_pairs = over_keys(
        backward_step, jnp.zeros((seqs, rows * heads, HEAD), jnp.float32)
    )
    if key_count != span:
        d_pairs = jnp.moveaxis(d_pairs, 0, 1)
    d_pairs = (
        d_pairs.reshape(seqs, high, low, rows, 2 * HEAD)
        .transpose(1, 2, 0, 3, 4)
        .reshape(high, low, count, 2 * HEAD)
    )
    near_sums = groups.sum_far([d_pairs[m] for m in range(high)]).astype(jnp.bfloat16)
    pair_grads = jnp.sum(groups.swap_near(near_sums).astype(jnp.float32), axis=0)
    d_rotated = jnp.concatenate(
        [d_query.reshape(count, heads, HEAD), pair_grads[:, None, :HEAD]], axis=1
    )
    d_lin = jnp.concatenate(
        [
            unrotate(d_rotated, cosine, sine).reshape(count, query_width + HEAD),
            pair_grads[:, HEAD:],
        ],
        axis=1,
    ).astype(jnp.bfloat16)
    d_normed = sum_tp(dot(d_lin, w_qkv, 1, 1).astype(jnp.bfloat16))
    d_input_norm, d_gain_one = norm_back(inputs, scale_one, gain_one, d_normed)
    tokens_grad = (d_hidden + d_input_norm).astype(jnp.bfloat16)
    d_w_attn = jnp.concatenate(
        [dot(normed_low, d_lin, 0, 0), dot(d_hidden_low, out_flat, 0, 0)], axis=1
    ).astype(jnp.bfloat16)
    d_w_attn = lax.psum_scatter(d_w_attn, "ctx", scatter_dimension=0, tiled=True).astype(
        jnp.float32
    )
    sums = jnp.concatenate([d_gain_one, d_gain_two, jnp.sum(d_lin.astype(jnp.float32), axis=0)])
    sums = jnp.sum(groups.gather_near(sums[None]), axis=0)
    sums = jnp.sum(groups.from_far(sums), axis=0)
    g_one = lax.dynamic_slice_in_dim(sums, device * share, share, 0)
    g_two = lax.dynamic_slice_in_dim(sums, width + device * share, share, 0)
    g_bias = sums[2 * width :]
    return (
        mixed.reshape(tokens.shape),
        tokens_grad.reshape(tokens.shape),
        g_one,
        g_two,
        d_w_attn[:, :query_width],
        d_w_attn[:, query_width : query_width + HEAD],
        d_w_attn[:, query_width + HEAD : qkv_width],
        g_bias[:query_width],
        g_bias[query_width : query_width + HEAD],
        g_bias[query_width + HEAD :],
        d_w_attn[:, qkv_width:].T,
        g_gate,
        g_up,
        g_down,
    )


def solution(mesh):
    placed = (
        P(None, "ctx", None),
        P(None, "ctx", None),
        P(),
        P("ctx"),
        P("ctx"),
        P("ctx", "tp"),
        P("ctx", "tp"),
        P("ctx", "tp"),
        P("tp"),
        P("tp"),
        P("tp"),
        P("tp", "ctx"),
        P("ctx", "tp"),
        P("ctx", "tp"),
        P("tp", "ctx"),
    )
    return jax.shard_map(
        local,
        mesh=mesh,
        in_specs=placed,
        out_specs=(
            P(None, "ctx", None),
            P(None, "ctx", None),
            P("ctx"),
            P("ctx"),
            P("ctx", "tp"),
            P("ctx", "tp"),
            P("ctx", "tp"),
            P("tp"),
            P("tp"),
            P("tp"),
            P("tp", "ctx"),
            P("ctx", "tp"),
            P("ctx", "tp"),
            P("tp", "ctx"),
        ),
        check_vma=False,
    )
```

```python
import functools

import jax
import jax.numpy as jnp
from jax import lax
from jax.experimental import pallas as pl
from jax.experimental.pallas import tpu as pltpu
from jax.sharding import PartitionSpec as P

HEAD = 64


EPSILON = 1e-06
ROPE_BASE = 1000000.0
MASKED = -1e30
LOWEST = -1e29
VMEM_LIMIT = 48 * 1024 * 1024


def rope_tables(positions, head_dim):
    halfway = head_dim // 2
    inverse = ROPE_BASE ** (-(jnp.arange(halfway, dtype=jnp.float32) * 2.0 / head_dim))
    angles = positions.astype(jnp.float32)[..., None] * inverse
    angles = jnp.concatenate([angles, angles], axis=-1)
    return (jnp.cos(angles), jnp.sin(angles))


def unrotate(grads, cosine, sine):
    halfway = grads.shape[-1] // 2
    moved = grads * sine
    back = jnp.concatenate([moved[..., halfway:], -moved[..., :halfway]], axis=-1)
    return grads * cosine + back


def norm_apply(values):
    factor = lax.rsqrt(jnp.mean(values * values, axis=-1, keepdims=True) + EPSILON)
    return values * factor, factor


def norm_back(values, factor, weighted):
    inner = jnp.mean(weighted * values, axis=-1, keepdims=True)
    return factor * weighted - values * factor * factor * factor * inner


def dot(left, right, left_dim, right_dim):
    return lax.dot_general(
        left, right, (((left_dim,), (right_dim,)), ((), ())), preferred_element_type=jnp.float32
    )


def sum_tp(values):
    other = lax.ppermute(values, "tp", [(0, 1), (1, 0)])
    return values.astype(jnp.float32) + other.astype(jnp.float32)


def together(*values):
    return lax.optimization_barrier(values)


class Groups:
    def __init__(self, count):
        self.count = count
        self.low = min(4, count)
        self.high = count // self.low
        self.near = [[h * self.low + k for k in range(self.low)] for h in range(self.high)]
        self.far = [list(group) for group in zip(*self.near)]

    def flip(self, values, bit):
        return lax.ppermute(values, "ctx", [(i, i ^ bit) for i in range(self.count)])

    def swap_near(self, values):
        return lax.all_to_all(values, "ctx", 0, 0, tiled=True, axis_index_groups=self.near)

    def gather_near(self, values):
        first = jnp.concatenate([values, self.flip(values, 2)], axis=0)
        return first, self.flip(first, 1)

    def sum_near(self, parts):
        kept = parts[0].astype(jnp.float32) + self.flip(parts[1], 1).astype(jnp.float32)
        kept = kept.astype(jnp.bfloat16)
        rows = kept.shape[0] // 2
        sent = self.flip(kept[rows:], 2)
        return (kept[:rows].astype(jnp.float32) + sent.astype(jnp.float32)).astype(jnp.bfloat16)

    def far_flips(self, values):
        return [values] + [self.flip(values, self.low * m) for m in range(1, self.high)]

    def gather_far(self, values, place):
        if self.high != 4:
            return lax.all_gather(values, "ctx", axis=0, axis_index_groups=self.far)
        group = place // self.low
        far = jnp.stack(self.far_flips(values)).reshape((2, 2) + values.shape)
        far = jnp.where(group // 2 % 2 == 1, far[::-1], far)
        far = jnp.where(group % 2 == 1, far[:, ::-1], far)
        return far.reshape((4,) + values.shape)

    def spread_near(self, values):
        whole = lax.all_gather(values, "ctx", axis=0, axis_index_groups=self.near)
        whole = jnp.swapaxes(whole, 0, 1)
        return whole.reshape((self.count * values.shape[1],) + values.shape[2:])

    def gather_xor(self, values):
        far = jnp.stack(self.far_flips(values))
        both = jnp.stack([far, self.flip(far, 2)])
        return jnp.stack([both, self.flip(both, 1)])

    def sum_xor(self, pieces):
        kept = pieces[0].astype(jnp.float32) + self.flip(pieces[1], 1).astype(jnp.float32)
        low = kept.astype(jnp.bfloat16)
        kept = kept[0] + self.flip(low[1], 2).astype(jnp.float32)
        low = kept.astype(jnp.bfloat16)
        total = kept[0]
        for m in range(1, self.high):
            total = total + self.flip(low[m], self.low * m).astype(jnp.float32)
        return total

    def near_owner(self, pieces, place):
        pieces = pieces.reshape((self.high, 2, 2) + pieces.shape[1:])
        return halve(self, halve(self, pieces, 1, place, 2), 2, place, 1)

    def far_owner(self, pieces, place):
        if self.high > 4:
            shape = pieces.shape
            pieces = pieces.reshape((shape[0] * shape[1],) + shape[2:])
            return lax.psum_scatter(
                pieces, "ctx", scatter_dimension=0, tiled=True, axis_index_groups=self.far
            ).astype(jnp.float32)
        group = place // self.low
        total = lax.dynamic_index_in_dim(pieces, group, 0, False).astype(jnp.float32)
        for m in range(1, self.high):
            sent = lax.dynamic_index_in_dim(pieces, group ^ m, 0, False)
            total = total + self.flip(sent, self.low * m).astype(jnp.float32)
        return total


def halve(groups, pieces, bit, place, axis):
    mine = place // bit % 2
    kept = lax.dynamic_index_in_dim(pieces, mine, axis, False).astype(jnp.float32)
    sent = groups.flip(lax.dynamic_index_in_dim(pieces, 1 - mine, axis, False), bit)
    return (kept + sent.astype(jnp.float32)).astype(jnp.bfloat16)


def stack_heads(flat, heads, upper):
    tall = jnp.concatenate([flat[:, h * HEAD : (h + 1) * HEAD] for h in range(heads)], axis=0)
    blank = jnp.zeros_like(tall)
    return jnp.concatenate([blank, tall] if upper else [tall, blank], axis=1)


def flat_heads(tall, heads):
    rows = tall.shape[0] // heads
    return jnp.concatenate([tall[h * rows : (h + 1) * rows] for h in range(heads)], axis=1)


def masked_scores(pair, wide, key_pos, query_pos):
    return jnp.where(key_pos <= query_pos, dot(pair, wide, 1, 1), MASKED)


def first_half(shape):
    return lax.broadcasted_iota(jnp.int32, shape, 1) % HEAD < HEAD // 2


def turn(values):
    width = values.shape[1]
    return jnp.where(
        first_half(values.shape),
        pltpu.roll(values, width - HEAD // 2, 1),
        pltpu.roll(values, HEAD // 2, 1),
    )


def widen(table, width):
    return jnp.concatenate([table] * (width // table.shape[1]), axis=1)


def project_kernel(
    heads, token_ref, w_ref, bias_ref, cosine_ref, sine_ref, normed_ref, query_ref, pair_ref
):
    normed, _ = norm_apply(token_ref[...].astype(jnp.float32))
    normed = normed.astype(jnp.bfloat16)
    normed_ref[...] = normed
    lin = dot(normed, w_ref[...], 1, 0) + bias_ref[...]
    width = (heads + 1) * HEAD
    some = lin[:, :width]
    turned = turn(some)
    turned = jnp.where(first_half(some.shape), -turned, turned)
    rotated = some * widen(cosine_ref[...], width) + turned * widen(sine_ref[...], width)
    rotated = rotated.astype(jnp.bfloat16)
    query_ref[...] = rotated[:, : heads * HEAD] * jnp.bfloat16(HEAD ** (-0.5))
    pair_ref[...] = jnp.concatenate(
        [rotated[:, heads * HEAD :], lin[:, width:].astype(jnp.bfloat16)], axis=1
    )


def load_pair(pair_ref):
    return pair_ref[...].reshape(-1, 2 * HEAD)


def forward_kernel(
    heads,
    query_ref,
    pair_ref,
    key_pos_ref,
    query_pos_ref,
    w_out_ref,
    flat_ref,
    part_ref,
    out_ref,
    log_ref,
    best_ref,
    total_ref,
    sum_ref,
):
    step = pl.program_id(1)

    @pl.when(step == 0)
    def _():
        best_ref[...] = jnp.full_like(best_ref, LOWEST)
        total_ref[...] = jnp.zeros_like(total_ref)
        sum_ref[...] = jnp.zeros_like(sum_ref)

    pair = load_pair(pair_ref)
    wide = stack_heads(query_ref[0], heads, False)
    scores = masked_scores(pair, wide, key_pos_ref[0], query_pos_ref[0])
    best = best_ref[...]
    newest = jnp.maximum(best, jnp.max(scores, axis=0, keepdims=True))
    raised = jnp.exp(scores - newest)
    fading = jnp.exp(best - newest)
    best_ref[...] = newest
    total_ref[...] = total_ref[...] * fading + jnp.sum(raised, axis=0, keepdims=True)
    sum_ref[...] = sum_ref[...] * fading + dot(pair, raised.astype(jnp.bfloat16), 0, 0)

    @pl.when(step == pl.num_programs(1) - 1)
    def _():
        out = sum_ref[HEAD:, :] / total_ref[...]
        out_ref[0] = out
        log_ref[0] = best_ref[...] + jnp.log(total_ref[...])
        flat = flat_heads(out.T, heads).astype(jnp.bfloat16)
        flat_ref[0] = flat
        part_ref[0] = dot(flat, w_out_ref[...], 1, 1).astype(jnp.bfloat16)


def backward_kernel(
    heads,
    query_ref,
    pair_ref,
    key_pos_ref,
    query_pos_ref,
    out_ref,
    log_ref,
    w_out_ref,
    own_ref,
    other_ref,
    hidden_ref,
    cotangent_ref,
    cosine_ref,
    sine_ref,
    d_hidden_ref,
    d_low_ref,
    d_query_ref,
    d_pair_ref,
    d_out_ref,
    dots_ref,
    sum_ref,
):
    step = pl.program_id(1)

    @pl.when(step == 0)
    def _():
        sum_ref[...] = jnp.zeros_like(sum_ref)
        hidden = hidden_ref[0]
        weighted = own_ref[0].astype(jnp.float32) + other_ref[0].astype(jnp.float32)
        _, scale = norm_apply(hidden)
        d_hidden = cotangent_ref[0].astype(jnp.float32) + norm_back(hidden, scale, weighted)
        d_hidden_ref[0] = d_hidden
        low = d_hidden.astype(jnp.bfloat16)
        d_low_ref[0] = low
        flat = dot(low, w_out_ref[...], 1, 0).astype(jnp.bfloat16)
        d_out = stack_heads(flat, heads, True)
        d_out_ref[...] = d_out
        dots_ref[...] = jnp.sum(
            d_out[:, HEAD:].astype(jnp.float32).T * out_ref[0], axis=0, keepdims=True
        )

    pair = load_pair(pair_ref)
    wide = stack_heads(query_ref[0], heads, False)
    d_out = d_out_ref[...]
    scores = masked_scores(pair, wide, key_pos_ref[0], query_pos_ref[0])
    chances = jnp.exp(scores - log_ref[0])
    d_scores = (chances * (dot(pair, d_out, 1, 1) - dots_ref[...])).astype(jnp.bfloat16)
    d_pair = dot(d_scores, wide, 1, 0) + dot(chances.astype(jnp.bfloat16), d_out, 1, 0)
    d_pair_ref[...] = d_pair.astype(jnp.bfloat16).reshape(d_pair_ref.shape)
    sum_ref[...] += dot(pair, d_scores, 0, 0)

    @pl.when(step == pl.num_programs(1) - 1)
    def _():
        flat = flat_heads(sum_ref[:HEAD, :].T, heads) * (HEAD ** (-0.5))
        width = (heads + 1) * HEAD
        flat = jnp.concatenate([flat, jnp.zeros((flat.shape[0], HEAD), jnp.float32)], axis=1)
        turned = turn(flat * widen(sine_ref[0], width))
        turned = jnp.where(first_half(flat.shape), turned, -turned)
        back = flat * widen(cosine_ref[0], width) + turned
        d_query_ref[0] = back[:, : heads * HEAD].astype(jnp.bfloat16)


def attention_call(kernel, name, heads, rows, ctx, seqs, width, inputs, kinds, outs, scratch):
    group = min(ctx, 1024 // rows)
    span = group * rows
    tall = heads * rows
    wide = heads * HEAD
    shapes = {
        "flat": ((seqs, rows, wide), (1, rows, wide), lambda s, k: (s, 0, 0)),
        "model": ((seqs, rows, width), (1, rows, width), lambda s, k: (s, 0, 0)),
        "table": ((seqs, rows, 2 * HEAD), (1, rows, 2 * HEAD), lambda s, k: (s, 0, 0)),
        "pair": (
            (ctx, seqs, rows, 2 * HEAD),
            (group, 1, rows, 2 * HEAD),
            lambda s, k: (k, s, 0, 0),
        ),
        "key": ((seqs, ctx * rows, 1), (1, span, 1), lambda s, k: (s, k, 0)),
        "row": ((seqs, 1, tall), (1, 1, tall), lambda s, k: (s, 0, 0)),
        "out": ((seqs, HEAD, tall), (1, HEAD, tall), lambda s, k: (s, 0, 0)),
        "weight": ((width, wide), (width, wide), lambda s, k: (0, 0)),
    }
    spec = lambda kind: pl.BlockSpec(shapes[kind][1], shapes[kind][2])
    flops = 2 * seqs * tall * ctx * rows * 2 * HEAD * (2 if name == "forward" else 5)
    return pl.pallas_call(
        functools.partial(kernel, heads),
        grid=(seqs, ctx // group),
        in_specs=[spec(kind) for kind in kinds],
        out_specs=[spec(kind) for kind, _ in outs],
        out_shape=[jax.ShapeDtypeStruct(shapes[kind][0], dtype) for kind, dtype in outs],
        scratch_shapes=scratch,
        compiler_params=pltpu.CompilerParams(
            dimension_semantics=("arbitrary", "arbitrary"), vmem_limit_bytes=VMEM_LIMIT
        ),
        cost_estimate=pl.CostEstimate(
            flops=flops,
            bytes_accessed=4 * seqs * ctx * rows * 2 * HEAD,
            transcendentals=seqs * tall * ctx * rows,
        ),
        name=name,
    )(*inputs)


def ffn_kernel(
    part,
    normed_one,
    normed_two,
    grad_one,
    grad_two,
    w_ref,
    near_ref,
    mixed_ref,
    active_ref,
    d_gate_up_ref,
):
    step = pl.program_id(0)

    def run(normed_ref, grad_ref):
        gate_up = dot(normed_ref[...], w_ref[:, : 2 * part], 1, 0)
        gate, up_values = gate_up[:, :part], gate_up[:, part:]
        sigma = 1.0 / (1.0 + jnp.exp(-gate))
        silu = gate * sigma
        active = (silu * up_values).astype(jnp.bfloat16)
        active_ref[...] = active
        d_active = dot(grad_ref[...], w_ref[:, 2 * part :], 1, 0)
        d_gate = d_active * up_values * sigma * (1.0 + gate * (1.0 - sigma))
        d_gate_up = jnp.concatenate([d_gate, d_active * silu], axis=1).astype(jnp.bfloat16)
        d_gate_up_ref[...] = d_gate_up
        near_ref[0] = dot(d_gate_up, w_ref[:, : 2 * part], 1, 1).astype(jnp.bfloat16)
        mixed_ref[0] = dot(active, w_ref[:, 2 * part :], 1, 1).astype(jnp.bfloat16)

    pl.when(step == 0)(functools.partial(run, normed_one, grad_one))
    pl.when(step == 1)(functools.partial(run, normed_two, grad_two))


def ffn_call(part, normed, grads, w_ffn):
    block, width = normed[0].shape
    fixed = lambda shape: pl.BlockSpec(shape, lambda i: (0, 0))
    model = pl.BlockSpec((1, block, width), lambda i: (i, 0, 0))
    units = lambda count: pl.BlockSpec((block, count * part), lambda i: (i, 0))
    return pl.pallas_call(
        functools.partial(ffn_kernel, part),
        grid=(2,),
        in_specs=[fixed((block, width))] * 4 + [fixed(w_ffn.shape)],
        out_specs=[model, model, units(1), units(2)],
        out_shape=[
            jax.ShapeDtypeStruct((2, block, width), jnp.bfloat16),
            jax.ShapeDtypeStruct((2, block, width), jnp.bfloat16),
            jax.ShapeDtypeStruct((2 * block, part), jnp.bfloat16),
            jax.ShapeDtypeStruct((2 * block, 2 * part), jnp.bfloat16),
        ],
        compiler_params=pltpu.CompilerParams(
            dimension_semantics=("arbitrary",), vmem_limit_bytes=VMEM_LIMIT
        ),
        cost_estimate=pl.CostEstimate(
            flops=4 * block * width * part * 6,
            bytes_accessed=2 * width * (8 * block + 3 * part),
            transcendentals=2 * block * part,
        ),
        name="ffn",
    )(*normed, *grads, w_ffn)


def ffn_grad_kernel(
    normed_one, normed_two, grad_one, grad_two, active_ref, d_gate_up_ref, out_ref
):
    step = pl.program_id(0)

    def run(one_ref, two_ref, right_ref):
        half = one_ref.shape[0]
        total = dot(one_ref[...], right_ref[:half], 0, 0) + dot(two_ref[...], right_ref[half:], 0, 0)
        out_ref[...] = total.astype(jnp.bfloat16)

    pl.when(step < 2)(functools.partial(run, normed_one, normed_two, d_gate_up_ref))
    pl.when(step == 2)(functools.partial(run, grad_one, grad_two, active_ref))


def ffn_grad_call(part, normed, grads, active, d_gate_up):
    block, width = normed[0].shape
    fixed = lambda shape: pl.BlockSpec(shape, lambda j: (0, 0))
    return pl.pallas_call(
        ffn_grad_kernel,
        grid=(3,),
        in_specs=[fixed((block, width))] * 4
        + [
            fixed((2 * block, part)),
            pl.BlockSpec((2 * block, part), lambda j: (0, jnp.minimum(j, 1))),
        ],
        out_specs=pl.BlockSpec((width, part), lambda j: (0, j)),
        out_shape=jax.ShapeDtypeStruct((width, 3 * part), jnp.bfloat16),
        compiler_params=pltpu.CompilerParams(
            dimension_semantics=("arbitrary",), vmem_limit_bytes=VMEM_LIMIT
        ),
        cost_estimate=pl.CostEstimate(
            flops=4 * block * width * part * 3,
            bytes_accessed=2 * width * (8 * block + 3 * part),
            transcendentals=0,
        ),
        name="ffn_grad",
    )(*normed, *grads, active, d_gate_up)


def local(
    tokens,
    cotangent,
    block_of,
    norm_gain,
    ffn_gain,
    w_query,
    w_key,
    w_value,
    b_query,
    b_key,
    b_value,
    w_out,
    w_gate,
    w_up,
    w_down,
):
    seqs, rows, width = tokens.shape
    count = seqs * rows
    block_len = rows // 2
    ctx = lax.axis_size("ctx")
    groups = Groups(ctx)
    low = groups.low
    device = lax.axis_index("ctx")
    heads = w_query.shape[1] // HEAD
    share = width // ctx
    units = w_gate.shape[1]
    part = -(-units // (low * 128)) * 128
    query_width = heads * HEAD
    own_gain_one = norm_gain.astype(jnp.float32)[:, None]
    own_gain_two = ffn_gain.astype(jnp.float32)[:, None]

    def scaled(matrix, gain):
        return (matrix.astype(jnp.float32) * gain).astype(jnp.bfloat16)

    def pieces(matrix):
        return jnp.pad(matrix, ((0, 0), (0, low * part - units))).reshape(share, low, part)

    w_ffn = jnp.concatenate(
        [
            pieces(scaled(w_gate, own_gain_two)),
            pieces(scaled(w_up, own_gain_two)),
            pieces(w_down.T),
        ],
        axis=2,
    )
    w_ffn = groups.swap_near(w_ffn.transpose(1, 0, 2)).reshape(low * share, 3 * part)
    w_attn = jnp.concatenate(
        [scaled(jnp.concatenate([w_query, w_key, w_value], axis=1), own_gain_one), w_out.T], axis=1
    )
    w_attn = groups.gather_far(w_attn, device)

    offsets = jnp.arange(block_len, dtype=jnp.int32)
    own_blocks = lax.dynamic_slice_in_dim(block_of, device * 2, 2, 1)
    row_pos = (own_blocks[:, :, None] * block_len + offsets).reshape(seqs, rows)
    query_pos = jnp.tile(row_pos, (1, heads))[:, None, :]
    flips = jnp.arange(ctx, dtype=jnp.int32)
    high = groups.high
    flips = flips // (2 * high) + flips // high % 2 * 2 + flips % high * low
    key_blocks = block_of.reshape(seqs, ctx, 2)[:, device ^ flips]
    key_pos = (key_blocks[..., None] * block_len + offsets).reshape(seqs, ctx * rows, 1)
    cosine, sine = rope_tables(row_pos.reshape(count), HEAD)
    cosine, sine = jnp.tile(cosine, (1, 2)), jnp.tile(sine, (1, 2))

    w_ffn, w_attn, key_pos, query_pos, cosine, sine = together(
        w_ffn, w_attn, key_pos, query_pos, cosine, sine
    )
    w_ffn = lax.all_gather(w_ffn, "ctx", axis=0, tiled=True, axis_index_groups=groups.far)
    qkv_width = query_width + 2 * HEAD
    w_qkv = groups.spread_near(w_attn[:, :, :qkv_width])
    grads_in = cotangent.reshape(count, width)

    bias = jnp.concatenate([b_query, b_key, b_value]).astype(jnp.float32)[None]
    normed_low, queries, pair = pl.pallas_call(
        functools.partial(project_kernel, heads),
        out_shape=[
            jax.ShapeDtypeStruct((count, width), jnp.bfloat16),
            jax.ShapeDtypeStruct((count, query_width), jnp.bfloat16),
            jax.ShapeDtypeStruct((count, 2 * HEAD), jnp.bfloat16),
        ],
        compiler_params=pltpu.CompilerParams(vmem_limit_bytes=VMEM_LIMIT),
        cost_estimate=pl.CostEstimate(
            flops=2 * count * width * (query_width + 2 * HEAD),
            bytes_accessed=2 * width * (count + query_width),
            transcendentals=0,
        ),
        name="project",
    )(tokens.reshape(count, width), w_qkv, bias, cosine, sine)
    queries = queries.reshape(seqs, rows, query_width)
    pairs = groups.gather_xor(pair).reshape(ctx, seqs, rows, 2 * HEAD)
    w_out_t = groups.spread_near(w_attn[:, :, qkv_width:])
    pairs, w_out_t = together(pairs, w_out_t)
    attend = functools.partial(
        attention_call, heads=heads, rows=rows, ctx=ctx, seqs=seqs, width=width
    )
    tall = heads * rows
    out_flat, attention, out_tall, log_total = attend(
        forward_kernel,
        "forward",
        inputs=(queries, pairs, key_pos, query_pos, w_out_t),
        kinds=("flat", "pair", "key", "row", "weight"),
        outs=(
            ("flat", jnp.bfloat16),
            ("model", jnp.bfloat16),
            ("out", jnp.float32),
            ("row", jnp.float32),
        ),
        scratch=[
            pltpu.VMEM((1, tall), jnp.float32),
            pltpu.VMEM((1, tall), jnp.float32),
            pltpu.VMEM((2 * HEAD, tall), jnp.float32),
        ],
    )
    out_flat = out_flat.reshape(count, query_width)
    inputs = tokens.astype(jnp.float32).reshape(count, width)
    hidden = inputs + sum_tp(attention.reshape(count, width))

    grads_near = groups.gather_near(grads_in)
    hidden, *grads_near = together(hidden, *grads_near)
    normed_two, _ = norm_apply(hidden)
    near_two = groups.gather_near(normed_two.astype(jnp.bfloat16))
    d_near, mixed_near, active, d_gate_up = ffn_call(part, near_two, grads_near, w_ffn)
    d_w_ffn = ffn_grad_call(part, near_two, grads_near, active, d_gate_up)
    d_own = groups.sum_near(d_near)
    d_own, _ = together(d_own, d_w_ffn)
    d_other = lax.ppermute(d_own, "tp", [(0, 1), (1, 0)])
    d_w_ffn = lax.psum_scatter(
        d_w_ffn, "ctx", scatter_dimension=0, tiled=True, axis_index_groups=groups.far
    )

    by_seq = lambda values: values.reshape((seqs, rows) + values.shape[1:])
    d_hidden, d_hidden_low, d_query_low, d_pairs = attend(
        backward_kernel,
        "backward",
        inputs=(
            queries,
            pairs,
            key_pos,
            query_pos,
            out_tall,
            log_total,
            w_out_t,
            by_seq(d_own),
            by_seq(d_other),
            by_seq(hidden),
            cotangent,
            by_seq(cosine),
            by_seq(sine),
        ),
        kinds=(
            ("flat", "pair", "key", "row", "out", "row", "weight")
            + ("model", "model", "model", "model", "table", "table")
        ),
        outs=(
            ("model", jnp.float32),
            ("model", jnp.bfloat16),
            ("flat", jnp.bfloat16),
            ("pair", jnp.bfloat16),
        ),
        scratch=[
            pltpu.VMEM((tall, 2 * HEAD), jnp.bfloat16),
            pltpu.VMEM((1, tall), jnp.float32),
            pltpu.VMEM((2 * HEAD, tall), jnp.float32),
        ],
    )
    d_hidden = d_hidden.reshape(count, width)
    d_hidden_low = d_hidden_low.reshape(count, width)
    d_query_low = d_query_low.reshape(count, query_width)
    mixed_near, d_query_low = together(mixed_near, d_query_low)
    mixed_own = groups.sum_near(mixed_near)
    pair_grads = groups.sum_xor(d_pairs.reshape(2, 2, high, count, 2 * HEAD))
    d_w_wide = jnp.concatenate(
        [dot(normed_low, d_query_low, 0, 0), dot(d_hidden_low, out_flat, 0, 0)], axis=1
    ).astype(jnp.bfloat16)
    d_w_wide = groups.near_owner(d_w_wide.reshape(ctx, share, 2 * query_width), device)
    pair_grads, mixed_own, d_w_wide = together(pair_grads, mixed_own, d_w_wide)
    d_w_wide = groups.far_owner(d_w_wide, device)
    mixed = (hidden + sum_tp(mixed_own)).astype(jnp.bfloat16)

    d_key = pair_grads[:, :HEAD]
    d_pair_low = jnp.concatenate(
        [unrotate(d_key, cosine[:, :HEAD], sine[:, :HEAD]), pair_grads[:, HEAD:]], axis=1
    ).astype(jnp.bfloat16)
    d_weighted_part = dot(d_query_low, w_qkv[:, :query_width], 1, 1) + dot(
        d_pair_low, w_qkv[:, query_width:], 1, 1
    )
    d_weighted = sum_tp(d_weighted_part.astype(jnp.bfloat16))
    normed, scale_one = norm_apply(inputs)
    tokens_grad = (d_hidden + norm_back(inputs, scale_one, d_weighted)).astype(jnp.bfloat16)

    d_weighted_two = d_own.astype(jnp.float32) + d_other.astype(jnp.float32)
    ones = jnp.zeros((2, count, 128), jnp.float32)
    ones = ones.at[0, :, 0].set(1.0).at[1, :, 1].set(1.0).reshape(2 * count, 128)
    gain_columns = lax.dot_general(
        jnp.concatenate([d_weighted_part * normed, d_weighted_two * normed_two], axis=0),
        ones,
        (((0,), (0,)), ((), ())),
        precision=lax.Precision.HIGHEST,
    )
    narrow = jnp.concatenate([dot(normed_low, d_pair_low, 0, 0), gain_columns], axis=1)
    bias = jnp.concatenate(
        [
            jnp.sum(d_query_low.astype(jnp.float32), axis=0),
            jnp.sum(d_pair_low.astype(jnp.float32), axis=0),
        ]
    )
    bias = jnp.pad(bias, (0, 8 * 256 - bias.shape[0])).reshape(1, 8, 256)
    narrow = jnp.concatenate(
        [narrow.reshape(ctx, share, 256), jnp.broadcast_to(bias, (ctx, 8, 256))], axis=1
    ).astype(jnp.bfloat16)
    narrow = groups.far_owner(groups.near_owner(narrow, device), device)
    d_w_ffn = groups.swap_near(d_w_ffn.reshape(low, share, 3 * part))
    d_w_ffn = d_w_ffn.transpose(1, 0, 2).astype(jnp.float32)

    def whole(index):
        some = d_w_ffn[:, :, index * part : (index + 1) * part]
        return some.reshape(share, low * part)[:, :units]

    g_gate, g_up, g_down = whole(0) * own_gain_two, whole(1) * own_gain_two, whole(2).T

    g_bias = narrow[share:].reshape(8 * 256)
    g_pair = narrow[:share, : 2 * HEAD] * own_gain_one
    g_two = narrow[:share, 2 * HEAD + 1] / own_gain_two[:, 0]
    g_one = narrow[:share, 2 * HEAD] / own_gain_one[:, 0]
    g_one = g_one + lax.ppermute(g_one, "tp", [(0, 1), (1, 0)])
    return (
        mixed.reshape(tokens.shape),
        tokens_grad.reshape(tokens.shape),
        g_one,
        g_two,
        d_w_wide[:, :query_width] * own_gain_one,
        g_pair[:, :HEAD],
        g_pair[:, HEAD:],
        g_bias[:query_width],
        g_bias[query_width : query_width + HEAD],
        g_bias[query_width + HEAD : query_width + 2 * HEAD],
        d_w_wide[:, query_width:].T,
        g_gate,
        g_up,
        g_down,
    )


def solution(mesh):
    placed = (
        P(None, "ctx", None),
        P(None, "ctx", None),
        P(),
        P("ctx"),
        P("ctx"),
        P("ctx", "tp"),
        P("ctx", "tp"),
        P("ctx", "tp"),
        P("tp"),
        P("tp"),
        P("tp"),
        P("tp", "ctx"),
        P("ctx", "tp"),
        P("ctx", "tp"),
        P("tp", "ctx"),
    )
    return jax.shard_map(
        local,
        mesh=mesh,
        in_specs=placed,
        out_specs=(
            P(None, "ctx", None),
            P(None, "ctx", None),
            P("ctx"),
            P("ctx"),
            P("ctx", "tp"),
            P("ctx", "tp"),
            P("ctx", "tp"),
            P("tp"),
            P("tp"),
            P("tp"),
            P("tp", "ctx"),
            P("ctx", "tp"),
            P("ctx", "tp"),
            P("tp", "ctx"),
        ),
        check_vma=False,
    )
```

```python
import functools

import jax
import jax.numpy as jnp
from jax import lax
from jax.experimental import pallas as pl
from jax.experimental.pallas import tpu as pltpu
from jax.sharding import PartitionSpec as P

HEAD = 64


EPSILON = 1e-06
ROPE_BASE = 1000000.0
MASKED = -1e30
LOWEST = -1e29
BRIEF = pl.CostEstimate(flops=1, bytes_accessed=1, transcendentals=0)
VMEM_LIMIT = 48 * 1024 * 1024


def rope_tables(positions, head_dim):
    halfway = head_dim // 2
    inverse = ROPE_BASE ** (-(jnp.arange(halfway, dtype=jnp.float32) * 2.0 / head_dim))
    angles = positions.astype(jnp.float32)[..., None] * inverse
    angles = jnp.concatenate([angles, angles], axis=-1)
    return (jnp.cos(angles), jnp.sin(angles))


def norm_apply(values):
    factor = lax.rsqrt(jnp.mean(values * values, axis=-1, keepdims=True) + EPSILON)
    return values * factor, factor


def norm_back(values, factor, weighted):
    inner = jnp.mean(weighted * values, axis=-1, keepdims=True)
    return factor * weighted - values * factor * factor * factor * inner


def dot(left, right, left_dim, right_dim):
    return lax.dot_general(
        left, right, (((left_dim,), (right_dim,)), ((), ())), preferred_element_type=jnp.float32
    )


def sum_tp(values):
    other = lax.ppermute(values, "tp", [(0, 1), (1, 0)])
    return values.astype(jnp.float32) + other.astype(jnp.float32)


def together(*values):
    return lax.optimization_barrier(values)


class Groups:
    def __init__(self, count):
        self.count = count
        self.low = 4
        self.high = count // self.low
        self.near = [[base + here for here in range(4)] for base in range(0, count, 4)]
        self.far = [list(group) for group in zip(*self.near)]
        self.far_bits = list(range(0, count, 4))

    def flip(self, values, bit):
        return lax.ppermute(values, "ctx", [(i, i ^ bit) for i in range(self.count)])

    def swap_near(self, values):
        return lax.all_to_all(values, "ctx", 0, 0, tiled=True, axis_index_groups=self.near)

    def gather_near(self, values):
        first = jnp.concatenate([values, self.flip(values, 2)], axis=0)
        return first, self.flip(first, 1)

    def far_flips(self, values):
        return jnp.stack([values] + [self.flip(values, bits) for bits in self.far_bits[1:]])


    def gather_far(self, values, place):
        if self.high != 4:
            return lax.all_gather(values, "ctx", axis=0, axis_index_groups=self.far)
        far = self.far_flips(values).reshape((2, 2) + values.shape)
        far = jnp.where(place // 8 % 2 == 1, far[::-1], far)
        far = jnp.where(place // 4 % 2 == 1, far[:, ::-1], far)
        return far.reshape((4,) + values.shape)

    def spread_near(self, values):
        whole = lax.all_gather(values, "ctx", axis=0, axis_index_groups=self.near)
        whole = jnp.swapaxes(whole, 0, 1)
        return whole.reshape((self.count * values.shape[1],) + values.shape[2:])

    def flip_near(self, values, place):
        other = self.flip(values, 2)
        upper = place // 2 % 2 == 1
        both = jnp.stack([jnp.where(upper, other, values), jnp.where(upper, values, other)], axis=1)
        other = self.flip(both, 1)
        upper = place % 2 == 1
        whole = jnp.stack([jnp.where(upper, other, both), jnp.where(upper, both, other)], axis=2)
        return whole.reshape((self.count * values.shape[1],) + values.shape[2:])

    def far_owner(self, pieces, place):
        if self.high != 4:
            shape = pieces.shape
            pieces = pieces.reshape((shape[0] * shape[1],) + shape[2:])
            return lax.psum_scatter(
                pieces, "ctx", scatter_dimension=0, tiled=True, axis_index_groups=self.far
            ).astype(jnp.float32)
        group = place // self.low
        total = lax.dynamic_index_in_dim(pieces, group, 0, False).astype(jnp.float32)
        for m in range(1, self.high):
            sent = lax.dynamic_index_in_dim(pieces, group ^ m, 0, False)
            total = total + self.flip(sent, self.far_bits[m]).astype(jnp.float32)
        return total


def add(one, two):
    return (one.astype(jnp.float32) + two.astype(jnp.float32)).astype(jnp.bfloat16)


def halve(groups, pieces, bit, place, axis):
    mine = place // bit % 2
    kept = lax.dynamic_index_in_dim(pieces, mine, axis, False).astype(jnp.float32)
    sent = groups.flip(lax.dynamic_index_in_dim(pieces, 1 - mine, axis, False), bit)
    return (kept + sent.astype(jnp.float32)).astype(jnp.bfloat16)


def stack_heads(flat, heads, upper):
    tall = jnp.concatenate([flat[:, h * HEAD : (h + 1) * HEAD] for h in range(heads)], axis=0)
    blank = jnp.zeros_like(tall)
    return jnp.concatenate([blank, tall] if upper else [tall, blank], axis=1)


def flat_heads(tall, heads):
    rows = tall.shape[0] // heads
    return jnp.concatenate([tall[h * rows : (h + 1) * rows] for h in range(heads)], axis=1)


def masked_scores(pair, wide, key_pos, query_pos):
    return jnp.where(key_pos <= query_pos, dot(pair, wide, 1, 1), MASKED)


def first_half(shape):
    return lax.broadcasted_iota(jnp.int32, shape, 1) % HEAD < HEAD // 2


def turn(values):
    width = values.shape[1]
    return jnp.where(
        first_half(values.shape),
        pltpu.roll(values, width - HEAD // 2, 1),
        pltpu.roll(values, HEAD // 2, 1),
    )


def widen(table, width):
    return jnp.concatenate([table] * (width // table.shape[1]), axis=1)


def project_kernel(
    heads, token_ref, w_ref, bias_ref, cosine_ref, sine_ref, normed_ref, query_ref, pair_ref
):
    normed, _ = norm_apply(token_ref[...].astype(jnp.float32))
    normed = normed.astype(jnp.bfloat16)
    normed_ref[...] = normed
    lin = dot(normed, w_ref[...], 1, 0) + bias_ref[...]
    width = (heads + 1) * HEAD
    some = lin[:, :width]
    turned = turn(some)
    turned = jnp.where(first_half(some.shape), -turned, turned)
    rotated = some * widen(cosine_ref[...], width) + turned * widen(sine_ref[...], width)
    rotated = rotated.astype(jnp.bfloat16)
    query_ref[...] = rotated[:, : heads * HEAD] * jnp.bfloat16(HEAD ** (-0.5))
    pair_ref[...] = jnp.concatenate(
        [rotated[:, heads * HEAD :], lin[:, width:].astype(jnp.bfloat16)], axis=1
    )


def whole_call(kernel, name, inputs, out_shape, scratch=(), place=None):
    whole = pl.BlockSpec(memory_space=pltpu.VMEM)
    in_specs = [whole] * len(inputs)
    if place is not None:
        inputs = (place.astype(jnp.int32)[None], *inputs)
        in_specs = [pl.BlockSpec(memory_space=pltpu.SMEM)] + in_specs
    return pl.pallas_call(
        kernel,
        in_specs=in_specs,
        out_specs=[whole] * len(out_shape),
        out_shape=out_shape,
        scratch_shapes=list(scratch),
        compiler_params=pltpu.CompilerParams(vmem_limit_bytes=VMEM_LIMIT),
        cost_estimate=BRIEF,
        name=name,
    )(*inputs)


def when(flag):
    if isinstance(flag, bool):
        return lambda body: body() if flag else None
    return pl.when(flag)


def forward_kernel(
    heads,
    steps,
    query_ref,
    pair_ref,
    key_pos_ref,
    query_pos_ref,
    w_out_ref,
    flat_ref,
    part_ref,
    out_ref,
    log_ref,
    best_ref,
    total_ref,
    sum_ref,
):
    step = 0 if steps == 1 else pl.program_id(1)
    for s in range(query_ref.shape[0]):

        @when(step == 0)
        def _():
            best_ref[s] = jnp.full(best_ref.shape[1:], LOWEST, jnp.float32)
            total_ref[s] = jnp.zeros(total_ref.shape[1:], jnp.float32)
            sum_ref[s] = jnp.zeros(sum_ref.shape[1:], jnp.float32)

        pair = pair_ref[:, s].reshape(-1, 2 * HEAD)
        wide = stack_heads(query_ref[s], heads, False)
        scores = masked_scores(pair, wide, key_pos_ref[s], query_pos_ref[s])
        best = best_ref[s]
        newest = jnp.maximum(best, jnp.max(scores, axis=0, keepdims=True))
        raised = jnp.exp(scores - newest)
        fading = jnp.exp(best - newest)
        best_ref[s] = newest
        total_ref[s] = total_ref[s] * fading + jnp.sum(raised, axis=0, keepdims=True)
        sum_ref[s] = sum_ref[s] * fading + dot(pair, raised.astype(jnp.bfloat16), 0, 0)

        @when(step == steps - 1)
        def _():
            out = sum_ref[s, HEAD:, :] / total_ref[s]
            if steps > 1:
                out_ref[s] = out
            log_ref[s] = best_ref[s] + jnp.log(total_ref[s])
            flat = flat_heads(out.T, heads).astype(jnp.bfloat16)
            flat_ref[s] = flat
            part_ref[s] = dot(flat, w_out_ref[...], 1, 1).astype(jnp.bfloat16)


def backward_kernel(
    heads,
    steps,
    query_ref,
    pair_ref,
    key_pos_ref,
    query_pos_ref,
    out_ref,
    log_ref,
    w_out_ref,
    own_ref,
    other_ref,
    hidden_ref,
    cotangent_ref,
    cosine_ref,
    sine_ref,
    d_hidden_ref,
    d_low_ref,
    d_query_ref,
    d_pair_ref,
    d_out_ref,
    dots_ref,
    sum_ref,
):
    step = 0 if steps == 1 else pl.program_id(1)
    for s in range(query_ref.shape[0]):

        @when(step == 0)
        def _():
            sum_ref[s] = jnp.zeros(sum_ref.shape[1:], jnp.float32)
            hidden = hidden_ref[s]
            weighted = own_ref[s].astype(jnp.float32) + other_ref[s].astype(jnp.float32)
            _, scale = norm_apply(hidden)
            d_hidden = cotangent_ref[s].astype(jnp.float32) + norm_back(hidden, scale, weighted)
            d_hidden_ref[s] = d_hidden
            low = d_hidden.astype(jnp.bfloat16)
            d_low_ref[s] = low
            flat = dot(low, w_out_ref[...], 1, 0).astype(jnp.bfloat16)
            d_out = stack_heads(flat, heads, True)
            d_out_ref[s] = d_out
            if steps > 1:
                dots_ref[s] = jnp.sum(
                    d_out[:, HEAD:].astype(jnp.float32).T * out_ref[s], axis=0, keepdims=True
                )

        pair = pair_ref[:, s].reshape(-1, 2 * HEAD)
        wide = stack_heads(query_ref[s], heads, False)
        d_out = d_out_ref[s]
        scores = masked_scores(pair, wide, key_pos_ref[s], query_pos_ref[s])
        chances = jnp.exp(scores - log_ref[s])
        d_chances = dot(pair, d_out, 1, 1)
        if steps > 1:
            dots = dots_ref[s]
        else:
            dots = jnp.sum(chances * d_chances, axis=0, keepdims=True)
        d_scores = (chances * (d_chances - dots)).astype(jnp.bfloat16)
        d_pair = dot(d_scores, wide, 1, 0) + dot(chances.astype(jnp.bfloat16), d_out, 1, 0)
        d_pair = d_pair.astype(jnp.bfloat16)
        d_pair_ref[:, s] = d_pair.reshape(d_pair_ref.shape[:1] + d_pair_ref.shape[2:])
        sum_ref[s] += dot(pair, d_scores, 0, 0)

        @when(step == steps - 1)
        def _():
            flat = flat_heads(sum_ref[s, :HEAD, :].T, heads) * (HEAD ** (-0.5))
            d_query_ref[s] = turn_back(flat, cosine_ref[s], sine_ref[s]).astype(jnp.bfloat16)


def turn_back(flat, cosine, sine):
    wide = -(-flat.shape[1] // 128) * 128
    blank = jnp.zeros((flat.shape[0], wide - flat.shape[1]), jnp.float32)
    padded = jnp.concatenate([flat, blank], axis=1) if wide > flat.shape[1] else flat
    turned = turn(padded * widen(sine, wide))
    turned = jnp.where(first_half(padded.shape), turned, -turned)
    return (padded * widen(cosine, wide) + turned)[:, : flat.shape[1]]


def attention_call(kernel, name, heads, rows, ctx, seqs, width, inputs, kinds, outs, scratch):
    group = min(ctx, 1024 // rows)
    steps = ctx // group
    span = group * rows
    tall = heads * rows
    wide = heads * HEAD
    shapes = {
        "flat": ((seqs, rows, wide), (1, rows, wide), lambda s, k: (s, 0, 0)),
        "model": ((seqs, rows, width), (1, rows, width), lambda s, k: (s, 0, 0)),
        "table": ((seqs, rows, 2 * HEAD), (1, rows, 2 * HEAD), lambda s, k: (s, 0, 0)),
        "pair": (
            (ctx, seqs, rows, 2 * HEAD),
            (group, 1, rows, 2 * HEAD),
            lambda s, k: (k, s, 0, 0),
        ),
        "key": ((seqs, ctx * rows, 1), (1, span, 1), lambda s, k: (s, k, 0)),
        "row": ((seqs, 1, tall), (1, 1, tall), lambda s, k: (s, 0, 0)),
        "out": ((seqs, HEAD, tall), (1, HEAD, tall), lambda s, k: (s, 0, 0)),
        "none": ((1, 8, 128), (1, 8, 128), lambda s, k: (0, 0, 0)),
        "weight": ((width, wide), (width, wide), lambda s, k: (0, 0)),
    }
    out_shape = [jax.ShapeDtypeStruct(shapes[kind][0], dtype) for kind, dtype in outs]
    here = seqs if steps == 1 else 1
    scratch = [pltpu.VMEM((here,) + shape, dtype) for shape, dtype in scratch]
    kernel = functools.partial(kernel, heads, steps)
    if steps == 1:
        return whole_call(kernel, name, inputs, out_shape, scratch)
    spec = lambda kind: pl.BlockSpec(shapes[kind][1], shapes[kind][2])
    return pl.pallas_call(
        kernel,
        grid=(seqs, steps),
        in_specs=[spec(kind) for kind in kinds],
        out_specs=[spec(kind) for kind, _ in outs],
        out_shape=out_shape,
        scratch_shapes=scratch,
        compiler_params=pltpu.CompilerParams(vmem_limit_bytes=VMEM_LIMIT),
        cost_estimate=BRIEF,
        name=name,
    )(*inputs)


def ffn_kernel(part, token_ref, w_ref, *refs):
    near_refs, mixed_refs, active_ref, d_gate_up_ref = refs[:2], refs[2:4], *refs[4:]
    block = token_ref.shape[0] // 4
    for half in (1, 0):
        rows = pl.ds(half * block, block)
        gate_up = dot(token_ref[rows, :], w_ref[:, : 2 * part], 1, 0)
        gate, up_values = gate_up[:, :part], gate_up[:, part:]
        sigma = 1.0 / (1.0 + jnp.exp(-gate))
        silu = gate * sigma
        active = (silu * up_values).astype(jnp.bfloat16)
        active_ref[rows, :] = active
        d_active = dot(token_ref[pl.ds((2 + half) * block, block), :], w_ref[:, 2 * part :], 1, 0)
        d_gate = d_active * up_values * sigma * (1.0 + gate * (1.0 - sigma))
        d_gate_up = jnp.concatenate([d_gate, d_active * silu], axis=1).astype(jnp.bfloat16)
        d_gate_up_ref[rows, :] = d_gate_up
        near_refs[half][...] = dot(d_gate_up, w_ref[:, : 2 * part], 1, 1).astype(jnp.bfloat16)
        mixed_refs[half][...] = dot(active, w_ref[:, 2 * part :], 1, 1).astype(jnp.bfloat16)


def ffn_call(part, tokens, w_ffn):
    block, width = tokens.shape[0] // 4, tokens.shape[1]
    model = jax.ShapeDtypeStruct((block, width), jnp.bfloat16)
    units = lambda count: jax.ShapeDtypeStruct((2 * block, count * part), jnp.bfloat16)
    return whole_call(
        functools.partial(ffn_kernel, part),
        "ffn",
        (tokens, w_ffn),
        [model, model, model, model, units(1), units(2)],
    )


def ffn_grad_kernel(part, token_ref, active_ref, d_gate_up_ref, out_ref):
    half = token_ref.shape[0] // 2
    for index in range(3):
        columns = slice(index * part, (index + 1) * part)
        left = token_ref[:half, :] if index < 2 else token_ref[half:, :]
        right = d_gate_up_ref[:, columns] if index < 2 else active_ref[...]
        out_ref[:, columns] = dot(left, right, 0, 0).astype(jnp.bfloat16)


def ffn_grad_call(part, tokens, active, d_gate_up):
    return whole_call(
        functools.partial(ffn_grad_kernel, part),
        "ffn_grad",
        (tokens, active, d_gate_up),
        [jax.ShapeDtypeStruct((tokens.shape[1], 3 * part), jnp.bfloat16)],
    )[0]


def split_rows(total, place_ref, share, kept_ref, sent_ref):
    odd = place_ref[0] % 2 == 1
    for index in range(total.shape[0] // (2 * share)):
        even_rows = total[2 * index * share : (2 * index + 1) * share]
        odd_rows = total[(2 * index + 1) * share : (2 * index + 2) * share]
        kept_ref[index] = jnp.where(odd, odd_rows, even_rows).astype(jnp.bfloat16)
        sent_ref[index] = jnp.where(odd, even_rows, odd_rows).astype(jnp.bfloat16)


def wide_kernel(share, place_ref, normed_ref, d_query_ref, d_low_ref, flat_ref, kept_ref, sent_ref):
    d_query = dot(normed_ref[...], d_query_ref[...], 0, 0)
    d_w_out = dot(d_low_ref[...], flat_ref[...], 0, 0)
    split_rows(jnp.concatenate([d_query, d_w_out], axis=1), place_ref, share, kept_ref, sent_ref)


def finish_kernel(
    share,
    place_ref,
    pair_ref,
    cosine_ref,
    sine_ref,
    normed_ref,
    token_ref,
    w_ref,
    d_query_ref,
    own_ref,
    other_ref,
    hidden_ref,
    same_ref,
    column_ref,
    weighted_ref,
    kept_ref,
    sent_ref,
):
    pair = pair_ref[...]
    turned = turn_back(pair, cosine_ref[...], sine_ref[...])
    lane = lax.broadcasted_iota(jnp.int32, pair.shape, 1)
    d_pair = jnp.where(lane < HEAD, turned, pair).astype(jnp.bfloat16)
    d_lin = jnp.concatenate([d_query_ref[...], d_pair], axis=1)
    weighted = dot(d_lin, w_ref[...], 1, 1)
    weighted_ref[...] = weighted.astype(jnp.bfloat16)
    count = pair.shape[0]
    d_pair_w = dot(normed_ref[...], d_pair, 0, 0)
    normed, _ = norm_apply(token_ref[...].astype(jnp.float32))
    hidden, _ = norm_apply(hidden_ref[...])
    weighted_two = own_ref[...].astype(jnp.float32) + other_ref[...].astype(jnp.float32)

    def spot(column):
        return (lax.broadcasted_iota(jnp.int32, (count, 128), 1) == column).astype(jnp.bfloat16)

    gains = dot((weighted * normed).astype(jnp.bfloat16), spot(0), 0, 0)
    gains = gains + dot((weighted_two * hidden).astype(jnp.bfloat16), spot(1), 0, 0)
    ones = jnp.ones((count, 128), jnp.bfloat16)
    bias = dot(d_lin, ones, 0, 0)
    bias = jnp.where(column_ref[...] > 0, bias, 0.0).astype(jnp.bfloat16)
    bias = dot(same_ref[...], bias, 1, 0)
    total = jnp.concatenate([d_pair_w, gains + bias], axis=1)
    split_rows(total, place_ref, share, kept_ref, sent_ref)


def local(
    tokens,
    cotangent,
    block_of,
    norm_gain,
    ffn_gain,
    w_query,
    w_key,
    w_value,
    b_query,
    b_key,
    b_value,
    w_out,
    w_gate,
    w_up,
    w_down,
):
    seqs, rows, width = tokens.shape
    count = seqs * rows
    block_len = rows // 2
    ctx = lax.axis_size("ctx")
    groups = Groups(ctx)
    low = groups.low
    device = lax.axis_index("ctx")
    heads = w_query.shape[1] // HEAD
    share = width // ctx
    units = w_gate.shape[1]
    part = -(-units // (low * 128)) * 128
    query_width = heads * HEAD
    own_gain_one = norm_gain.astype(jnp.float32)[:, None]
    own_gain_two = ffn_gain.astype(jnp.float32)[:, None]

    def scaled(matrix, gain):
        return (matrix.astype(jnp.float32) * gain).astype(jnp.bfloat16)

    def pieces(matrix):
        return jnp.pad(matrix, ((0, 0), (0, low * part - units))).reshape(share, low, part)

    w_ffn = jnp.concatenate(
        [
            pieces(scaled(w_gate, own_gain_two)),
            pieces(scaled(w_up, own_gain_two)),
            pieces(w_down.T),
        ],
        axis=2,
    ).transpose(1, 0, 2)
    w_attn = jnp.concatenate(
        [scaled(jnp.concatenate([w_query, w_key, w_value], axis=1), own_gain_one), w_out.T], axis=1
    )
    w_ffn, w_attn = together(w_ffn, w_attn)
    w_ffn = groups.swap_near(w_ffn).reshape(low * share, 3 * part)
    w_attn = groups.gather_far(w_attn, device)

    offsets = jnp.arange(block_len, dtype=jnp.int32)
    own_blocks = lax.dynamic_slice_in_dim(block_of, device * 2, 2, 1)
    row_pos = (own_blocks[:, :, None] * block_len + offsets).reshape(seqs, rows)
    query_pos = jnp.tile(row_pos, (1, heads))[:, None, :]
    flips = jnp.array(
        [core + step + far for core in (0, 1) for step in (0, 2) for far in groups.far_bits],
        jnp.int32,
    )
    key_blocks = block_of.reshape(seqs, ctx, 2)[:, device ^ flips]
    key_pos = (key_blocks[..., None] * block_len + offsets).reshape(seqs, ctx * rows, 1)
    cosine, sine = rope_tables(row_pos.reshape(count), HEAD)
    cosine, sine = jnp.tile(cosine, (1, 2)), jnp.tile(sine, (1, 2))

    w_ffn, w_attn, key_pos, query_pos, cosine, sine = together(
        w_ffn, w_attn, key_pos, query_pos, cosine, sine
    )
    w_ffn = lax.all_gather(w_ffn, "ctx", axis=0, tiled=True, axis_index_groups=groups.far)
    qkv_width = query_width + 2 * HEAD
    w_qkv = groups.spread_near(w_attn[:, :, :qkv_width])
    grads_in = cotangent.reshape(count, width)

    bias = jnp.concatenate([b_query, b_key, b_value]).astype(jnp.float32)[None]
    normed_low, queries, pair = whole_call(
        functools.partial(project_kernel, heads),
        "project",
        (tokens.reshape(count, width), w_qkv, bias, cosine, sine),
        [
            jax.ShapeDtypeStruct((count, width), jnp.bfloat16),
            jax.ShapeDtypeStruct((count, query_width), jnp.bfloat16),
            jax.ShapeDtypeStruct((count, 2 * HEAD), jnp.bfloat16),
        ],
    )
    queries = queries.reshape(seqs, rows, query_width)
    pairs = groups.far_flips(pair)
    w_out_t = groups.flip_near(w_attn[:, :, qkv_width:], device)
    pairs = jnp.stack([pairs, groups.flip(pairs, 2)])
    pairs = jnp.stack([pairs, groups.flip(pairs, 1)]).reshape(ctx, seqs, rows, 2 * HEAD)
    pairs, w_out_t = together(pairs, w_out_t)
    attend = functools.partial(
        attention_call, heads=heads, rows=rows, ctx=ctx, seqs=seqs, width=width
    )
    tall = heads * rows
    tall_kind = "out" if ctx * rows > 1024 else "none"
    out_flat, attention, out_tall, log_total = attend(
        forward_kernel,
        "forward",
        inputs=(queries, pairs, key_pos, query_pos, w_out_t),
        kinds=("flat", "pair", "key", "row", "weight"),
        outs=(
            ("flat", jnp.bfloat16),
            ("model", jnp.bfloat16),
            (tall_kind, jnp.float32),
            ("row", jnp.float32),
        ),
        scratch=[
            ((1, tall), jnp.float32),
            ((1, tall), jnp.float32),
            ((2 * HEAD, tall), jnp.float32),
        ],
    )
    out_flat = out_flat.reshape(count, query_width)
    inputs = tokens.astype(jnp.float32).reshape(count, width)
    hidden = inputs + sum_tp(attention.reshape(count, width))

    grads_near = groups.gather_near(grads_in)
    hidden, *grads_near = together(hidden, *grads_near)
    normed_two, _ = norm_apply(hidden)
    near_two = groups.gather_near(normed_two.astype(jnp.bfloat16))
    token_parts = jnp.concatenate([*near_two, *grads_near], axis=0)
    near_kept, near_sent, mixed_kept, mixed_sent, active, d_gate_up = ffn_call(
        part, token_parts, w_ffn
    )
    d_w_ffn = ffn_grad_call(part, token_parts, active, d_gate_up)
    crossed = groups.flip(near_sent, 1)
    crossed, d_w_ffn = together(crossed, d_w_ffn)
    d_w_ffn = lax.psum_scatter(
        d_w_ffn, "ctx", scatter_dimension=0, tiled=True, axis_index_groups=groups.far
    )
    near_sent = groups.flip(add(near_kept[count:], crossed[count:]), 2)
    d_own = add(add(near_kept[:count], crossed[:count]), near_sent)
    mixed_sent = groups.flip(mixed_sent, 1)
    d_own, mixed_sent = together(d_own, mixed_sent)
    d_other = lax.ppermute(d_own, "tp", [(0, 1), (1, 0)])
    mixed_kept = add(mixed_kept, mixed_sent)
    d_other, mixed_kept = together(d_other, mixed_kept)
    mixed_own = add(mixed_kept[:count], groups.flip(mixed_kept[count:], 2))

    by_seq = lambda values: values.reshape((seqs, rows) + values.shape[1:])
    d_hidden, d_hidden_low, d_query_low, d_pairs = attend(
        backward_kernel,
        "backward",
        inputs=(
            queries,
            pairs,
            key_pos,
            query_pos,
            out_tall,
            log_total,
            w_out_t,
            by_seq(d_own),
            by_seq(d_other),
            by_seq(hidden),
            cotangent,
            by_seq(cosine),
            by_seq(sine),
        ),
        kinds=(
            ("flat", "pair", "key", "row", tall_kind, "row", "weight")
            + ("model", "model", "model", "model", "table", "table")
        ),
        outs=(
            ("model", jnp.float32),
            ("model", jnp.bfloat16),
            ("flat", jnp.bfloat16),
            ("pair", jnp.bfloat16),
        ),
        scratch=[
            ((tall, 2 * HEAD), jnp.bfloat16),
            ((1, tall), jnp.float32),
            ((2 * HEAD, tall), jnp.float32),
        ],
    )
    d_hidden = d_hidden.reshape(count, width)
    d_hidden_low = d_hidden_low.reshape(count, width)
    d_query_low = d_query_low.reshape(count, query_width)
    d_pairs, mixed_own = together(d_pairs, mixed_own)
    mixed_other = lax.ppermute(mixed_own, "tp", [(0, 1), (1, 0)])
    d_pairs = d_pairs.reshape(2, 2 * groups.high * count, 2 * HEAD)
    crossed = groups.flip(d_pairs[1], 1)
    crossed, d_query_low = together(crossed, d_query_low)
    halves = lambda columns: [jax.ShapeDtypeStruct((ctx // 2, share, columns), jnp.bfloat16)] * 2
    wide_kept, wide_sent = whole_call(
        functools.partial(wide_kernel, share),
        "wide",
        (normed_low, d_query_low, d_hidden_low, out_flat),
        halves(2 * query_width),
        place=device,
    )
    wide_crossed = groups.flip(wide_sent, 1)
    d_pairs = add(d_pairs[0], crossed).reshape(2, groups.high * count, 2 * HEAD)
    d_pairs = add(d_pairs[0], groups.flip(d_pairs[1], 2)).reshape(groups.high, count, 2 * HEAD)
    d_pairs, wide_crossed = together(d_pairs, wide_crossed)
    near_half = lambda kept, crossed: halve(
        groups, add(kept, crossed).reshape((groups.high, 2) + kept.shape[1:]), 2, device, 1
    )
    d_w_wide = near_half(wide_kept, wide_crossed)
    pair_grads = d_pairs[0].astype(jnp.float32)
    for m in range(1, groups.high):
        pair_grads = pair_grads + groups.flip(d_pairs[m], groups.far_bits[m]).astype(jnp.float32)
    pair_grads, d_w_wide = together(pair_grads, d_w_wide)
    mixed = hidden + mixed_own.astype(jnp.float32) + mixed_other.astype(jnp.float32)
    mixed = mixed.astype(jnp.bfloat16)

    row = jnp.arange(width)[:, None] % share
    unit = jnp.arange(qkv_width)[None, :]
    same = (row == unit % share).astype(jnp.bfloat16)
    column = (unit.T // share + 2 == jnp.arange(128)[None, :]).astype(jnp.float32)
    d_weighted_low, narrow_kept, narrow_sent = whole_call(
        functools.partial(finish_kernel, share),
        "finish",
        (
            pair_grads,
            cosine,
            sine,
            normed_low,
            tokens.reshape(count, width),
            w_qkv,
            d_query_low,
            d_own,
            d_other,
            hidden,
            same,
            column,
        ),
        [
            jax.ShapeDtypeStruct((count, width), jnp.bfloat16),
            *halves(256),
        ],
        place=device,
    )
    d_weighted = sum_tp(d_weighted_low)
    _, scale_one = norm_apply(inputs)
    tokens_grad = (d_hidden + norm_back(inputs, scale_one, d_weighted)).astype(jnp.bfloat16)
    narrow = near_half(narrow_kept, groups.flip(narrow_sent, 1))
    narrow, d_w_ffn = together(jnp.concatenate([d_w_wide, narrow], axis=2), d_w_ffn)
    d_w_ffn = groups.swap_near(d_w_ffn.reshape(low, share, 3 * part))
    narrow = groups.far_owner(narrow, device)
    d_w_wide, narrow = narrow[:, : 2 * query_width], narrow[:, 2 * query_width :]

    def whole(swapped, index):
        some = swapped[:, :, index * part : (index + 1) * part].transpose(1, 0, 2)
        return some.reshape(share, low * part)[:, :units].astype(jnp.float32)

    g_gate = whole(d_w_ffn, 0) * own_gain_two
    g_up = whole(d_w_ffn, 1) * own_gain_two
    g_down = whole(d_w_ffn, 2).T

    held = -(-qkv_width // share)
    g_bias = narrow[:, 2 * HEAD + 2 : 2 * HEAD + 2 + held].T.reshape(held * share)
    g_pair = narrow[:, : 2 * HEAD] * own_gain_one
    g_two = narrow[:, 2 * HEAD + 1] / own_gain_two[:, 0]
    g_one = narrow[:, 2 * HEAD] / own_gain_one[:, 0]
    g_one = g_one + lax.ppermute(g_one, "tp", [(0, 1), (1, 0)])
    return (
        mixed.reshape(tokens.shape),
        tokens_grad.reshape(tokens.shape),
        g_one,
        g_two,
        d_w_wide[:, :query_width] * own_gain_one,
        g_pair[:, :HEAD],
        g_pair[:, HEAD:],
        g_bias[:query_width],
        g_bias[query_width : query_width + HEAD],
        g_bias[query_width + HEAD : query_width + 2 * HEAD],
        d_w_wide[:, query_width:].T,
        g_gate,
        g_up,
        g_down,
    )


def solution(mesh):
    placed = (
        P(None, "ctx", None),
        P(None, "ctx", None),
        P(),
        P("ctx"),
        P("ctx"),
        P("ctx", "tp"),
        P("ctx", "tp"),
        P("ctx", "tp"),
        P("tp"),
        P("tp"),
        P("tp"),
        P("tp", "ctx"),
        P("ctx", "tp"),
        P("ctx", "tp"),
        P("tp", "ctx"),
    )
    return jax.shard_map(
        local,
        mesh=mesh,
        in_specs=placed,
        out_specs=(
            P(None, "ctx", None),
            P(None, "ctx", None),
            P("ctx"),
            P("ctx"),
            P("ctx", "tp"),
            P("ctx", "tp"),
            P("ctx", "tp"),
            P("tp"),
            P("tp"),
            P("tp"),
            P("tp", "ctx"),
            P("ctx", "tp"),
            P("ctx", "tp"),
            P("tp", "ctx"),
        ),
        check_vma=False,
    )
```

```python
import functools

import jax
import jax.numpy as jnp
from jax import lax
from jax.experimental import pallas as pl
from jax.experimental.pallas import tpu as pltpu
from jax.sharding import PartitionSpec as P

HEAD = 64


EPSILON = 1e-06
ROPE_BASE = 1000000.0
MASKED = -1e30
LOWEST = -1e29
BRIEF = pl.CostEstimate(flops=1, bytes_accessed=1, transcendentals=0)
VMEM_LIMIT = 48 * 1024 * 1024
FFN_VMEM_LIMIT = 56 * 1024 * 1024


def rope_tables(positions, head_dim):
    halfway = head_dim // 2
    inverse = ROPE_BASE ** (-(jnp.arange(halfway, dtype=jnp.float32) * 2.0 / head_dim))
    angles = positions.astype(jnp.float32)[..., None] * inverse
    angles = jnp.concatenate([angles, angles], axis=-1)
    return (jnp.cos(angles), jnp.sin(angles))


def norm_apply(values):
    factor = lax.rsqrt(jnp.mean(values * values, axis=-1, keepdims=True) + EPSILON)
    return values * factor, factor


def norm_back(values, factor, weighted):
    inner = jnp.mean(weighted * values, axis=-1, keepdims=True)
    return factor * weighted - values * factor * factor * factor * inner


def dot(left, right, left_dim, right_dim):
    return lax.dot_general(
        left, right, (((left_dim,), (right_dim,)), ((), ())), preferred_element_type=jnp.float32
    )


def sum_tp(values):
    other = lax.ppermute(values, "tp", [(0, 1), (1, 0)])
    return values.astype(jnp.float32) + other.astype(jnp.float32)


def together(*values):
    return lax.optimization_barrier(values)


class Groups:
    def __init__(self, count):
        self.count = count
        self.low = 4
        self.high = count // self.low
        self.near = [[base + here for here in range(4)] for base in range(0, count, 4)]
        self.far = [list(group) for group in zip(*self.near)]
        self.far_bits = list(range(0, count, 4))

    def flip(self, values, bit):
        return lax.ppermute(values, "ctx", [(i, i ^ bit) for i in range(self.count)])

    def swap_near(self, values):
        return lax.all_to_all(values, "ctx", 0, 0, tiled=True, axis_index_groups=self.near)

    def gather_near(self, values):
        first = jnp.concatenate([values, self.flip(values, 2)], axis=0)
        return first, self.flip(first, 1)

    def far_flips(self, values):
        return jnp.stack([values] + [self.flip(values, bits) for bits in self.far_bits[1:]])


    def gather_far(self, values, place):
        if self.high != 4:
            return lax.all_gather(values, "ctx", axis=0, axis_index_groups=self.far)
        far = self.far_flips(values).reshape((2, 2) + values.shape)
        far = jnp.where(place // 8 % 2 == 1, far[::-1], far)
        far = jnp.where(place // 4 % 2 == 1, far[:, ::-1], far)
        return far.reshape((4,) + values.shape)

    def spread_near(self, values):
        whole = lax.all_gather(values, "ctx", axis=0, axis_index_groups=self.near)
        whole = jnp.swapaxes(whole, 0, 1)
        return whole.reshape((self.count * values.shape[1],) + values.shape[2:])

    def flip_near(self, values, place):
        other = self.flip(values, 2)
        upper = place // 2 % 2 == 1
        both = jnp.stack([jnp.where(upper, other, values), jnp.where(upper, values, other)], axis=1)
        other = self.flip(both, 1)
        upper = place % 2 == 1
        whole = jnp.stack([jnp.where(upper, other, both), jnp.where(upper, both, other)], axis=2)
        return whole.reshape((self.count * values.shape[1],) + values.shape[2:])

    def far_owner(self, pieces, place):
        if self.high != 4:
            shape = pieces.shape
            pieces = pieces.reshape((shape[0] * shape[1],) + shape[2:])
            return lax.psum_scatter(
                pieces, "ctx", scatter_dimension=0, tiled=True, axis_index_groups=self.far
            ).astype(jnp.float32)
        group = place // self.low
        total = lax.dynamic_index_in_dim(pieces, group, 0, False).astype(jnp.float32)
        for m in range(1, self.high):
            sent = lax.dynamic_index_in_dim(pieces, group ^ m, 0, False)
            total = total + self.flip(sent, self.far_bits[m]).astype(jnp.float32)
        return total


def add(one, two):
    return (one.astype(jnp.float32) + two.astype(jnp.float32)).astype(jnp.bfloat16)


def halve(groups, pieces, bit, place, axis):
    mine = place // bit % 2
    kept = lax.dynamic_index_in_dim(pieces, mine, axis, False).astype(jnp.float32)
    sent = groups.flip(lax.dynamic_index_in_dim(pieces, 1 - mine, axis, False), bit)
    return (kept + sent.astype(jnp.float32)).astype(jnp.bfloat16)


def stack_heads(flat, heads, upper):
    tall = jnp.concatenate([flat[:, h * HEAD : (h + 1) * HEAD] for h in range(heads)], axis=0)
    blank = jnp.zeros_like(tall)
    return jnp.concatenate([blank, tall] if upper else [tall, blank], axis=1)


def flat_heads(tall, heads):
    rows = tall.shape[0] // heads
    return jnp.concatenate([tall[h * rows : (h + 1) * rows] for h in range(heads)], axis=1)


def masked_scores(pair, wide, key_pos, query_pos):
    return jnp.where(key_pos <= query_pos, dot(pair, wide, 1, 1), MASKED)


def first_half(shape):
    return lax.broadcasted_iota(jnp.int32, shape, 1) % HEAD < HEAD // 2


def turn(values):
    width = values.shape[1]
    return jnp.where(
        first_half(values.shape),
        pltpu.roll(values, width - HEAD // 2, 1),
        pltpu.roll(values, HEAD // 2, 1),
    )


def widen(table, width):
    return jnp.concatenate([table] * (width // table.shape[1]), axis=1)


def project_kernel(
    heads, token_ref, w_ref, bias_ref, cosine_ref, sine_ref, normed_ref, query_ref, pair_ref
):
    normed, _ = norm_apply(token_ref[...].astype(jnp.float32))
    normed = normed.astype(jnp.bfloat16)
    normed_ref[...] = normed
    lin = dot(normed, w_ref[...], 1, 0) + bias_ref[...]
    width = (heads + 1) * HEAD
    some = lin[:, :width]
    turned = turn(some)
    turned = jnp.where(first_half(some.shape), -turned, turned)
    rotated = some * widen(cosine_ref[...], width) + turned * widen(sine_ref[...], width)
    rotated = rotated.astype(jnp.bfloat16)
    query_ref[...] = rotated[:, : heads * HEAD] * jnp.bfloat16(HEAD ** (-0.5))
    pair_ref[...] = jnp.concatenate(
        [rotated[:, heads * HEAD :], lin[:, width:].astype(jnp.bfloat16)], axis=1
    )


def whole_call(kernel, name, inputs, out_shape, scratch=(), place=None):
    whole = pl.BlockSpec(memory_space=pltpu.VMEM)
    in_specs = [whole] * len(inputs)
    if place is not None:
        inputs = (place.astype(jnp.int32)[None], *inputs)
        in_specs = [pl.BlockSpec(memory_space=pltpu.SMEM)] + in_specs
    return pl.pallas_call(
        kernel,
        in_specs=in_specs,
        out_specs=[whole] * len(out_shape),
        out_shape=out_shape,
        scratch_shapes=list(scratch),
        compiler_params=pltpu.CompilerParams(vmem_limit_bytes=VMEM_LIMIT),
        cost_estimate=BRIEF,
        name=name,
    )(*inputs)


def when(flag):
    if isinstance(flag, bool):
        return lambda body: body() if flag else None
    return pl.when(flag)


def forward_kernel(
    heads,
    steps,
    query_ref,
    pair_ref,
    key_pos_ref,
    query_pos_ref,
    w_out_ref,
    flat_ref,
    part_ref,
    out_ref,
    log_ref,
    best_ref,
    total_ref,
    sum_ref,
):
    step = 0 if steps == 1 else pl.program_id(1)
    for s in range(query_ref.shape[0]):

        @when(step == 0)
        def _():
            best_ref[s] = jnp.full(best_ref.shape[1:], LOWEST, jnp.float32)
            total_ref[s] = jnp.zeros(total_ref.shape[1:], jnp.float32)
            sum_ref[s] = jnp.zeros(sum_ref.shape[1:], jnp.float32)

        pair = pair_ref[:, s].reshape(-1, 2 * HEAD)
        wide = stack_heads(query_ref[s], heads, False)
        scores = masked_scores(pair, wide, key_pos_ref[s], query_pos_ref[s])
        best = best_ref[s]
        newest = jnp.maximum(best, jnp.max(scores, axis=0, keepdims=True))
        raised = jnp.exp(scores - newest)
        fading = jnp.exp(best - newest)
        best_ref[s] = newest
        total_ref[s] = total_ref[s] * fading + jnp.sum(raised, axis=0, keepdims=True)
        sum_ref[s] = sum_ref[s] * fading + dot(pair, raised.astype(jnp.bfloat16), 0, 0)

        @when(step == steps - 1)
        def _():
            out = sum_ref[s, HEAD:, :] / total_ref[s]
            if steps > 1:
                out_ref[s] = out
            log_ref[s] = best_ref[s] + jnp.log(total_ref[s])
            flat = flat_heads(out.T, heads).astype(jnp.bfloat16)
            flat_ref[s] = flat
            part_ref[s] = dot(flat, w_out_ref[...], 1, 1).astype(jnp.bfloat16)


def backward_kernel(
    heads,
    steps,
    query_ref,
    pair_ref,
    key_pos_ref,
    query_pos_ref,
    out_ref,
    log_ref,
    w_out_ref,
    own_ref,
    other_ref,
    hidden_ref,
    cotangent_ref,
    cosine_ref,
    sine_ref,
    d_hidden_ref,
    d_low_ref,
    d_query_ref,
    d_pair_ref,
    d_out_ref,
    dots_ref,
    sum_ref,
):
    step = 0 if steps == 1 else pl.program_id(1)
    for s in range(query_ref.shape[0]):

        @when(step == 0)
        def _():
            sum_ref[s] = jnp.zeros(sum_ref.shape[1:], jnp.float32)
            hidden = hidden_ref[s]
            weighted = own_ref[s].astype(jnp.float32) + other_ref[s].astype(jnp.float32)
            _, scale = norm_apply(hidden)
            d_hidden = cotangent_ref[s].astype(jnp.float32) + norm_back(hidden, scale, weighted)
            d_hidden_ref[s] = d_hidden
            low = d_hidden.astype(jnp.bfloat16)
            d_low_ref[s] = low
            flat = dot(low, w_out_ref[...], 1, 0).astype(jnp.bfloat16)
            d_out = stack_heads(flat, heads, True)
            d_out_ref[s] = d_out
            if steps > 1:
                dots_ref[s] = jnp.sum(
                    d_out[:, HEAD:].astype(jnp.float32).T * out_ref[s], axis=0, keepdims=True
                )

        pair = pair_ref[:, s].reshape(-1, 2 * HEAD)
        wide = stack_heads(query_ref[s], heads, False)
        d_out = d_out_ref[s]
        scores = masked_scores(pair, wide, key_pos_ref[s], query_pos_ref[s])
        chances = jnp.exp(scores - log_ref[s])
        d_chances = dot(pair, d_out, 1, 1)
        if steps > 1:
            dots = dots_ref[s]
        else:
            dots = jnp.sum(chances * d_chances, axis=0, keepdims=True)
        d_scores = (chances * (d_chances - dots)).astype(jnp.bfloat16)
        d_pair = dot(d_scores, wide, 1, 0) + dot(chances.astype(jnp.bfloat16), d_out, 1, 0)
        d_pair = d_pair.astype(jnp.bfloat16)
        d_pair_ref[:, s] = d_pair.reshape(d_pair_ref.shape[:1] + d_pair_ref.shape[2:])
        sum_ref[s] += dot(pair, d_scores, 0, 0)

        @when(step == steps - 1)
        def _():
            flat = flat_heads(sum_ref[s, :HEAD, :].T, heads) * (HEAD ** (-0.5))
            d_query_ref[s] = turn_back(flat, cosine_ref[s], sine_ref[s]).astype(jnp.bfloat16)


def turn_back(flat, cosine, sine):
    wide = -(-flat.shape[1] // 128) * 128
    blank = jnp.zeros((flat.shape[0], wide - flat.shape[1]), jnp.float32)
    padded = jnp.concatenate([flat, blank], axis=1) if wide > flat.shape[1] else flat
    turned = turn(padded * widen(sine, wide))
    turned = jnp.where(first_half(padded.shape), turned, -turned)
    return (padded * widen(cosine, wide) + turned)[:, : flat.shape[1]]


def attention_call(kernel, name, heads, rows, ctx, seqs, width, inputs, kinds, outs, scratch):
    group = min(ctx, 1024 // rows)
    steps = ctx // group
    span = group * rows
    tall = heads * rows
    wide = heads * HEAD
    shapes = {
        "flat": ((seqs, rows, wide), (1, rows, wide), lambda s, k: (s, 0, 0)),
        "model": ((seqs, rows, width), (1, rows, width), lambda s, k: (s, 0, 0)),
        "table": ((seqs, rows, 2 * HEAD), (1, rows, 2 * HEAD), lambda s, k: (s, 0, 0)),
        "pair": (
            (ctx, seqs, rows, 2 * HEAD),
            (group, 1, rows, 2 * HEAD),
            lambda s, k: (k, s, 0, 0),
        ),
        "key": ((seqs, ctx * rows, 1), (1, span, 1), lambda s, k: (s, k, 0)),
        "row": ((seqs, 1, tall), (1, 1, tall), lambda s, k: (s, 0, 0)),
        "out": ((seqs, HEAD, tall), (1, HEAD, tall), lambda s, k: (s, 0, 0)),
        "none": ((1, 8, 128), (1, 8, 128), lambda s, k: (0, 0, 0)),
        "weight": ((width, wide), (width, wide), lambda s, k: (0, 0)),
    }
    out_shape = [jax.ShapeDtypeStruct(shapes[kind][0], dtype) for kind, dtype in outs]
    here = seqs if steps == 1 else 1
    scratch = [pltpu.VMEM((here,) + shape, dtype) for shape, dtype in scratch]
    kernel = functools.partial(kernel, heads, steps)
    if steps == 1:
        return whole_call(kernel, name, inputs, out_shape, scratch)
    spec = lambda kind: pl.BlockSpec(shapes[kind][1], shapes[kind][2])
    return pl.pallas_call(
        kernel,
        grid=(seqs, steps),
        in_specs=[spec(kind) for kind in kinds],
        out_specs=[spec(kind) for kind, _ in outs],
        out_shape=out_shape,
        scratch_shapes=scratch,
        compiler_params=pltpu.CompilerParams(vmem_limit_bytes=VMEM_LIMIT),
        cost_estimate=BRIEF,
        name=name,
    )(*inputs)


def ffn_kernel(
    part,
    token_source,
    w_source,
    near_kept,
    near_sent,
    mixed_kept,
    mixed_sent,
    d_w_target,
    token_ref,
    w_ref,
    active_ref,
    d_gate_up_ref,
    grad_ref,
    model_ref,
    semaphores,
    sent_semaphores,
):
    models = (near_kept, near_sent, mixed_kept, mixed_sent)
    block = token_ref.shape[0] // 4
    gates = slice(0, 2 * part)
    downs = slice(2 * part, 3 * part)
    rows_of = lambda index: pl.ds(index * block, block)

    def load(source, target, index):
        copy = pltpu.make_async_copy(source, target, semaphores.at[index])
        copy.start()
        return copy

    copies = []

    def send(source, target):
        index = len(copies)
        copy = pltpu.make_async_copy(source, target, sent_semaphores.at[index])
        copy.start()
        copies.append(copy)

    def send_model(index, values):
        model_ref[index] = values.astype(jnp.bfloat16)
        send(model_ref.at[index], models[index])

    w_gates = load(w_source.at[:, gates], w_ref.at[:, gates], 4)
    tokens = {1: load(token_source.at[rows_of(1)], token_ref.at[rows_of(1)], 1)}
    tokens[3] = load(token_source.at[rows_of(3)], token_ref.at[rows_of(3)], 3)
    w_downs = load(w_source.at[:, downs], w_ref.at[:, downs], 5)
    for index in (0, 2):
        tokens[index] = load(token_source.at[rows_of(index)], token_ref.at[rows_of(index)], index)
    for half in (1, 0):
        rows = rows_of(half)
        tokens[half].wait()
        if half == 1:
            w_gates.wait()
        gate_up = dot(token_ref[rows, :], w_ref[:, gates], 1, 0)
        gate, up_values = gate_up[:, :part], gate_up[:, part:]
        sigma = 1.0 / (1.0 + jnp.exp(-gate))
        silu = gate * sigma
        active = (silu * up_values).astype(jnp.bfloat16)
        active_ref[rows, :] = active
        tokens[2 + half].wait()
        if half == 1:
            w_downs.wait()
        d_active = dot(token_ref[rows_of(2 + half), :], w_ref[:, downs], 1, 0)
        d_gate = d_active * up_values * sigma * (1.0 + gate * (1.0 - sigma))
        d_gate_up = jnp.concatenate([d_gate, d_active * silu], axis=1).astype(jnp.bfloat16)
        d_gate_up_ref[rows, :] = d_gate_up
        send_model(half, dot(d_gate_up, w_ref[:, gates], 1, 1))
        send_model(2 + half, dot(active, w_ref[:, downs], 1, 1))
    for index in range(3):
        columns = slice(index * part, (index + 1) * part)
        left = token_ref[: 2 * block, :] if index < 2 else token_ref[2 * block :, :]
        right = d_gate_up_ref[:, columns] if index < 2 else active_ref[...]
        grad_ref[:, columns] = dot(left, right, 0, 0).astype(jnp.bfloat16)
        send(grad_ref.at[:, columns], d_w_target.at[:, columns])
    for copy in copies:
        copy.wait()


def ffn_call(part, tokens, w_ffn):
    block, width = tokens.shape[0] // 4, tokens.shape[1]
    model = jax.ShapeDtypeStruct((block, width), jnp.bfloat16)
    far = pl.BlockSpec(memory_space=pltpu.HBM)
    return pl.pallas_call(
        functools.partial(ffn_kernel, part),
        in_specs=[far, far],
        out_specs=[far] * 5,
        out_shape=[model] * 4 + [jax.ShapeDtypeStruct(w_ffn.shape, jnp.bfloat16)],
        scratch_shapes=[
            pltpu.VMEM(tokens.shape, jnp.bfloat16),
            pltpu.VMEM(w_ffn.shape, jnp.bfloat16),
            pltpu.VMEM((2 * block, part), jnp.bfloat16),
            pltpu.VMEM((2 * block, 2 * part), jnp.bfloat16),
            pltpu.VMEM(w_ffn.shape, jnp.bfloat16),
            pltpu.VMEM((4, block, width), jnp.bfloat16),
            pltpu.SemaphoreType.DMA((6,)),
            pltpu.SemaphoreType.DMA((7,)),
        ],
        compiler_params=pltpu.CompilerParams(vmem_limit_bytes=FFN_VMEM_LIMIT),
        cost_estimate=BRIEF,
        name="ffn",
    )(tokens, w_ffn)


def split_rows(total, place_ref, share, kept_ref, sent_ref):
    odd = place_ref[0] % 2 == 1
    for index in range(total.shape[0] // (2 * share)):
        even_rows = total[2 * index * share : (2 * index + 1) * share]
        odd_rows = total[(2 * index + 1) * share : (2 * index + 2) * share]
        kept_ref[index] = jnp.where(odd, odd_rows, even_rows).astype(jnp.bfloat16)
        sent_ref[index] = jnp.where(odd, even_rows, odd_rows).astype(jnp.bfloat16)


def wide_kernel(share, place_ref, normed_ref, d_query_ref, d_low_ref, flat_ref, kept_ref, sent_ref):
    d_query = dot(normed_ref[...], d_query_ref[...], 0, 0)
    d_w_out = dot(d_low_ref[...], flat_ref[...], 0, 0)
    split_rows(jnp.concatenate([d_query, d_w_out], axis=1), place_ref, share, kept_ref, sent_ref)


def finish_kernel(
    share,
    place_ref,
    pair_ref,
    cosine_ref,
    sine_ref,
    normed_ref,
    token_ref,
    w_ref,
    d_query_ref,
    own_ref,
    other_ref,
    hidden_ref,
    same_ref,
    column_ref,
    weighted_ref,
    kept_ref,
    sent_ref,
):
    pair = pair_ref[...]
    turned = turn_back(pair, cosine_ref[...], sine_ref[...])
    lane = lax.broadcasted_iota(jnp.int32, pair.shape, 1)
    d_pair = jnp.where(lane < HEAD, turned, pair).astype(jnp.bfloat16)
    d_lin = jnp.concatenate([d_query_ref[...], d_pair], axis=1)
    weighted = dot(d_lin, w_ref[...], 1, 1)
    weighted_ref[...] = weighted.astype(jnp.bfloat16)
    count = pair.shape[0]
    d_pair_w = dot(normed_ref[...], d_pair, 0, 0)
    normed, _ = norm_apply(token_ref[...].astype(jnp.float32))
    hidden, _ = norm_apply(hidden_ref[...])
    weighted_two = own_ref[...].astype(jnp.float32) + other_ref[...].astype(jnp.float32)

    def spot(column):
        return (lax.broadcasted_iota(jnp.int32, (count, 128), 1) == column).astype(jnp.bfloat16)

    gains = dot((weighted * normed).astype(jnp.bfloat16), spot(0), 0, 0)
    gains = gains + dot((weighted_two * hidden).astype(jnp.bfloat16), spot(1), 0, 0)
    ones = jnp.ones((count, 128), jnp.bfloat16)
    bias = dot(d_lin, ones, 0, 0)
    bias = jnp.where(column_ref[...] > 0, bias, 0.0).astype(jnp.bfloat16)
    bias = dot(same_ref[...], bias, 1, 0)
    total = jnp.concatenate([d_pair_w, gains + bias], axis=1)
    split_rows(total, place_ref, share, kept_ref, sent_ref)


def local(
    tokens,
    cotangent,
    block_of,
    norm_gain,
    ffn_gain,
    w_query,
    w_key,
    w_value,
    b_query,
    b_key,
    b_value,
    w_out,
    w_gate,
    w_up,
    w_down,
):
    seqs, rows, width = tokens.shape
    count = seqs * rows
    block_len = rows // 2
    ctx = lax.axis_size("ctx")
    groups = Groups(ctx)
    low = groups.low
    device = lax.axis_index("ctx")
    heads = w_query.shape[1] // HEAD
    share = width // ctx
    units = w_gate.shape[1]
    part = -(-units // (low * 128)) * 128
    query_width = heads * HEAD
    own_gain_one = norm_gain.astype(jnp.float32)[:, None]
    own_gain_two = ffn_gain.astype(jnp.float32)[:, None]

    def scaled(matrix, gain):
        return (matrix.astype(jnp.float32) * gain).astype(jnp.bfloat16)

    def pieces(matrix):
        return jnp.pad(matrix, ((0, 0), (0, low * part - units))).reshape(share, low, part)

    w_ffn = jnp.concatenate(
        [
            pieces(scaled(w_gate, own_gain_two)),
            pieces(scaled(w_up, own_gain_two)),
            pieces(w_down.T),
        ],
        axis=2,
    ).transpose(1, 0, 2)
    w_attn = jnp.concatenate(
        [scaled(jnp.concatenate([w_query, w_key, w_value], axis=1), own_gain_one), w_out.T], axis=1
    )
    w_ffn, w_attn = together(w_ffn, w_attn)
    w_ffn = groups.swap_near(w_ffn).reshape(low * share, 3 * part)
    w_attn = groups.gather_far(w_attn, device)

    offsets = jnp.arange(block_len, dtype=jnp.int32)
    own_blocks = lax.dynamic_slice_in_dim(block_of, device * 2, 2, 1)
    row_pos = (own_blocks[:, :, None] * block_len + offsets).reshape(seqs, rows)
    query_pos = jnp.tile(row_pos, (1, heads))[:, None, :]
    flips = jnp.array(
        [core + step + far for core in (0, 1) for step in (0, 2) for far in groups.far_bits],
        jnp.int32,
    )
    key_blocks = block_of.reshape(seqs, ctx, 2)[:, device ^ flips]
    key_pos = (key_blocks[..., None] * block_len + offsets).reshape(seqs, ctx * rows, 1)
    cosine, sine = rope_tables(row_pos.reshape(count), HEAD)
    cosine, sine = jnp.tile(cosine, (1, 2)), jnp.tile(sine, (1, 2))

    qkv_width = query_width + 2 * HEAD
    row = jnp.arange(width)[:, None] % share
    unit = jnp.arange(qkv_width)[None, :]
    same = (row == unit % share).astype(jnp.bfloat16)
    column = (unit.T // share + 2 == jnp.arange(128)[None, :]).astype(jnp.float32)
    w_ffn, w_attn, key_pos, query_pos, cosine, sine, same, column = together(
        w_ffn, w_attn, key_pos, query_pos, cosine, sine, same, column
    )
    w_ffn = lax.all_gather(w_ffn, "ctx", axis=0, tiled=True, axis_index_groups=groups.far)
    w_qkv = groups.spread_near(w_attn[:, :, :qkv_width])
    grads_in = cotangent.reshape(count, width)

    bias = jnp.concatenate([b_query, b_key, b_value]).astype(jnp.float32)[None]
    normed_low, queries, pair = whole_call(
        functools.partial(project_kernel, heads),
        "project",
        (tokens.reshape(count, width), w_qkv, bias, cosine, sine),
        [
            jax.ShapeDtypeStruct((count, width), jnp.bfloat16),
            jax.ShapeDtypeStruct((count, query_width), jnp.bfloat16),
            jax.ShapeDtypeStruct((count, 2 * HEAD), jnp.bfloat16),
        ],
    )
    queries = queries.reshape(seqs, rows, query_width)
    pairs = groups.far_flips(pair)
    w_out_t = groups.flip_near(w_attn[:, :, qkv_width:], device)
    pairs = jnp.stack([pairs, groups.flip(pairs, 2)])
    pairs = jnp.stack([pairs, groups.flip(pairs, 1)]).reshape(ctx, seqs, rows, 2 * HEAD)
    pairs, w_out_t = together(pairs, w_out_t)
    attend = functools.partial(
        attention_call, heads=heads, rows=rows, ctx=ctx, seqs=seqs, width=width
    )
    tall = heads * rows
    tall_kind = "out" if ctx * rows > 1024 else "none"
    out_flat, attention, out_tall, log_total = attend(
        forward_kernel,
        "forward",
        inputs=(queries, pairs, key_pos, query_pos, w_out_t),
        kinds=("flat", "pair", "key", "row", "weight"),
        outs=(
            ("flat", jnp.bfloat16),
            ("model", jnp.bfloat16),
            (tall_kind, jnp.float32),
            ("row", jnp.float32),
        ),
        scratch=[
            ((1, tall), jnp.float32),
            ((1, tall), jnp.float32),
            ((2 * HEAD, tall), jnp.float32),
        ],
    )
    out_flat = out_flat.reshape(count, query_width)
    inputs = tokens.astype(jnp.float32).reshape(count, width)
    hidden = inputs + sum_tp(attention.reshape(count, width))

    grads_near = groups.gather_near(grads_in)
    hidden, *grads_near = together(hidden, *grads_near)
    normed_two, _ = norm_apply(hidden)
    near_two = groups.gather_near(normed_two.astype(jnp.bfloat16))
    token_parts = jnp.concatenate([*near_two, *grads_near], axis=0)
    near_kept, near_sent, mixed_kept, mixed_sent, d_w_ffn = ffn_call(part, token_parts, w_ffn)
    d_w_ffn = lax.psum_scatter(
        d_w_ffn, "ctx", scatter_dimension=0, tiled=True, axis_index_groups=groups.far
    )
    crossed = groups.flip(near_sent, 1)
    near_sent = groups.flip(add(near_kept[count:], crossed[count:]), 2)
    d_own = add(add(near_kept[:count], crossed[:count]), near_sent)
    mixed_sent = groups.flip(mixed_sent, 1)
    d_own, mixed_sent = together(d_own, mixed_sent)
    d_other = lax.ppermute(d_own, "tp", [(0, 1), (1, 0)])
    mixed_kept = add(mixed_kept, mixed_sent)
    d_other, mixed_kept = together(d_other, mixed_kept)
    mixed_own = add(mixed_kept[:count], groups.flip(mixed_kept[count:], 2))

    by_seq = lambda values: values.reshape((seqs, rows) + values.shape[1:])
    d_hidden, d_hidden_low, d_query_low, d_pairs = attend(
        backward_kernel,
        "backward",
        inputs=(
            queries,
            pairs,
            key_pos,
            query_pos,
            out_tall,
            log_total,
            w_out_t,
            by_seq(d_own),
            by_seq(d_other),
            by_seq(hidden),
            cotangent,
            by_seq(cosine),
            by_seq(sine),
        ),
        kinds=(
            ("flat", "pair", "key", "row", tall_kind, "row", "weight")
            + ("model", "model", "model", "model", "table", "table")
        ),
        outs=(
            ("model", jnp.float32),
            ("model", jnp.bfloat16),
            ("flat", jnp.bfloat16),
            ("pair", jnp.bfloat16),
        ),
        scratch=[
            ((tall, 2 * HEAD), jnp.bfloat16),
            ((1, tall), jnp.float32),
            ((2 * HEAD, tall), jnp.float32),
        ],
    )
    d_hidden = d_hidden.reshape(count, width)
    d_hidden_low = d_hidden_low.reshape(count, width)
    d_query_low = d_query_low.reshape(count, query_width)
    d_pairs, mixed_own = together(d_pairs, mixed_own)
    mixed_other = lax.ppermute(mixed_own, "tp", [(0, 1), (1, 0)])
    d_pairs = d_pairs.reshape(2, 2 * groups.high * count, 2 * HEAD)
    crossed = groups.flip(d_pairs[1], 1)
    crossed, d_query_low = together(crossed, d_query_low)
    halves = lambda columns: [jax.ShapeDtypeStruct((ctx // 2, share, columns), jnp.bfloat16)] * 2
    wide_kept, wide_sent = whole_call(
        functools.partial(wide_kernel, share),
        "wide",
        (normed_low, d_query_low, d_hidden_low, out_flat),
        halves(2 * query_width),
        place=device,
    )
    wide_crossed = groups.flip(wide_sent, 1)
    d_pairs = add(d_pairs[0], crossed).reshape(2, groups.high * count, 2 * HEAD)
    d_pairs = add(d_pairs[0], groups.flip(d_pairs[1], 2)).reshape(groups.high, count, 2 * HEAD)
    d_pairs, wide_crossed = together(d_pairs, wide_crossed)

    def near_half(kept, crossed):
        pieces = add(kept, crossed).reshape((groups.high, 2) + kept.shape[1:])
        mine = device // 2 % 2
        sent = lax.dynamic_index_in_dim(pieces, 1 - mine, 1, False)
        return lax.dynamic_index_in_dim(pieces, mine, 1, False), groups.flip(sent, 2)

    wide_kept, wide_beside = near_half(wide_kept, wide_crossed)
    pair_grads = d_pairs[0].astype(jnp.float32)
    for m in range(1, groups.high):
        pair_grads = pair_grads + groups.flip(d_pairs[m], groups.far_bits[m]).astype(jnp.float32)
    pair_grads, wide_beside = together(pair_grads, wide_beside)
    mixed = hidden + mixed_own.astype(jnp.float32) + mixed_other.astype(jnp.float32)
    mixed = mixed.astype(jnp.bfloat16)

    d_weighted_low, narrow_kept, narrow_sent = whole_call(
        functools.partial(finish_kernel, share),
        "finish",
        (
            pair_grads,
            cosine,
            sine,
            normed_low,
            tokens.reshape(count, width),
            w_qkv,
            d_query_low,
            d_own,
            d_other,
            hidden,
            same,
            column,
        ),
        [
            jax.ShapeDtypeStruct((count, width), jnp.bfloat16),
            *halves(256),
        ],
        place=device,
    )
    narrow_kept, narrow_beside = near_half(narrow_kept, groups.flip(narrow_sent, 1))
    narrow = jnp.concatenate(
        [add(wide_kept, wide_beside), add(narrow_kept, narrow_beside)], axis=2
    )
    narrow, d_w_ffn, d_weighted_low, mixed = together(narrow, d_w_ffn, d_weighted_low, mixed)
    d_weighted = sum_tp(d_weighted_low)
    _, scale_one = norm_apply(inputs)
    tokens_grad = (d_hidden + norm_back(inputs, scale_one, d_weighted)).astype(jnp.bfloat16)
    d_w_ffn = groups.swap_near(d_w_ffn.reshape(low, share, 3 * part))
    narrow = groups.far_owner(narrow, device)
    d_w_wide, narrow = narrow[:, : 2 * query_width], narrow[:, 2 * query_width :]

    def whole(swapped, index):
        some = swapped[:, :, index * part : (index + 1) * part].transpose(1, 0, 2)
        return some.reshape(share, low * part)[:, :units].astype(jnp.float32)

    g_gate = whole(d_w_ffn, 0) * own_gain_two
    g_up = whole(d_w_ffn, 1) * own_gain_two
    g_down = whole(d_w_ffn, 2).T

    held = -(-qkv_width // share)
    g_bias = narrow[:, 2 * HEAD + 2 : 2 * HEAD + 2 + held].T.reshape(held * share)
    g_pair = narrow[:, : 2 * HEAD] * own_gain_one
    g_two = narrow[:, 2 * HEAD + 1] / own_gain_two[:, 0]
    g_one = narrow[:, 2 * HEAD] / own_gain_one[:, 0]
    g_one = g_one + lax.ppermute(g_one, "tp", [(0, 1), (1, 0)])
    return (
        mixed.reshape(tokens.shape),
        tokens_grad.reshape(tokens.shape),
        g_one,
        g_two,
        d_w_wide[:, :query_width] * own_gain_one,
        g_pair[:, :HEAD],
        g_pair[:, HEAD:],
        g_bias[:query_width],
        g_bias[query_width : query_width + HEAD],
        g_bias[query_width + HEAD : query_width + 2 * HEAD],
        d_w_wide[:, query_width:].T,
        g_gate,
        g_up,
        g_down,
    )


def solution(mesh):
    placed = (
        P(None, "ctx", None),
        P(None, "ctx", None),
        P(),
        P("ctx"),
        P("ctx"),
        P("ctx", "tp"),
        P("ctx", "tp"),
        P("ctx", "tp"),
        P("tp"),
        P("tp"),
        P("tp"),
        P("tp", "ctx"),
        P("ctx", "tp"),
        P("ctx", "tp"),
        P("tp", "ctx"),
    )
    return jax.shard_map(
        local,
        mesh=mesh,
        in_specs=placed,
        out_specs=(
            P(None, "ctx", None),
            P(None, "ctx", None),
            P("ctx"),
            P("ctx"),
            P("ctx", "tp"),
            P("ctx", "tp"),
            P("ctx", "tp"),
            P("tp"),
            P("tp"),
            P("tp"),
            P("tp", "ctx"),
            P("ctx", "tp"),
            P("ctx", "tp"),
            P("tp", "ctx"),
        ),
        check_vma=False,
    )
```

```python
import functools

import jax
import jax.numpy as jnp
from jax import lax
from jax.experimental import pallas as pl
from jax.experimental.pallas import tpu as pltpu
from jax.sharding import PartitionSpec as P

HEAD = 64


EPSILON = 1e-06
ROPE_BASE = 1000000.0
MASKED = -1e30
LOWEST = -1e29
BRIEF = pl.CostEstimate(flops=1, bytes_accessed=1, transcendentals=0)
VMEM_LIMIT = 48 * 1024 * 1024
FFN_VMEM_LIMIT = 56 * 1024 * 1024


def rope_tables(positions, head_dim):
    halfway = head_dim // 2
    inverse = ROPE_BASE ** (-(jnp.arange(halfway, dtype=jnp.float32) * 2.0 / head_dim))
    angles = positions.astype(jnp.float32)[..., None] * inverse
    angles = jnp.concatenate([angles, angles], axis=-1)
    return (jnp.cos(angles), jnp.sin(angles))


def norm_apply(values):
    factor = lax.rsqrt(jnp.mean(values * values, axis=-1, keepdims=True) + EPSILON)
    return values * factor, factor


def norm_back(values, factor, weighted):
    inner = jnp.mean(weighted * values, axis=-1, keepdims=True)
    return factor * weighted - values * factor * factor * factor * inner


def dot(left, right, left_dim, right_dim):
    return lax.dot_general(
        left, right, (((left_dim,), (right_dim,)), ((), ())), preferred_element_type=jnp.float32
    )


def sum_tp(values):
    other = lax.ppermute(values, "tp", [(0, 1), (1, 0)])
    return values.astype(jnp.float32) + other.astype(jnp.float32)


def together(*values):
    return lax.optimization_barrier(values)


class Groups:
    def __init__(self, count):
        self.count = count
        self.low = 4
        self.high = count // self.low
        self.near = [[base + here for here in range(4)] for base in range(0, count, 4)]
        self.far = [list(group) for group in zip(*self.near)]
        self.far_bits = list(range(0, count, 4))

    def flip(self, values, bit):
        return lax.ppermute(values, "ctx", [(i, i ^ bit) for i in range(self.count)])

    def swap_near(self, values):
        return lax.all_to_all(values, "ctx", 0, 0, tiled=True, axis_index_groups=self.near)

    def gather_near(self, values):
        first = jnp.concatenate([values, self.flip(values, 2)], axis=0)
        return first, self.flip(first, 1)

    def far_flips(self, values):
        return jnp.stack([values] + [self.flip(values, bits) for bits in self.far_bits[1:]])


    def gather_far(self, values, place):
        if self.high != 4:
            return lax.all_gather(values, "ctx", axis=0, axis_index_groups=self.far)
        far = self.far_flips(values).reshape((2, 2) + values.shape)
        far = jnp.where(place // 8 % 2 == 1, far[::-1], far)
        far = jnp.where(place // 4 % 2 == 1, far[:, ::-1], far)
        return far.reshape((4,) + values.shape)

    def spread_near(self, values):
        whole = lax.all_gather(values, "ctx", axis=0, axis_index_groups=self.near)
        whole = jnp.swapaxes(whole, 0, 1)
        return whole.reshape((self.count * values.shape[1],) + values.shape[2:])

    def flip_near(self, values, place):
        other = self.flip(values, 2)
        upper = place // 2 % 2 == 1
        both = jnp.stack([jnp.where(upper, other, values), jnp.where(upper, values, other)], axis=1)
        other = self.flip(both, 1)
        upper = place % 2 == 1
        whole = jnp.stack([jnp.where(upper, other, both), jnp.where(upper, both, other)], axis=2)
        return whole.reshape((self.count * values.shape[1],) + values.shape[2:])

    def far_owner(self, pieces, place):
        if self.high != 4:
            shape = pieces.shape
            pieces = pieces.reshape((shape[0] * shape[1],) + shape[2:])
            return lax.psum_scatter(
                pieces, "ctx", scatter_dimension=0, tiled=True, axis_index_groups=self.far
            ).astype(jnp.float32)
        group = place // self.low
        total = lax.dynamic_index_in_dim(pieces, group, 0, False).astype(jnp.float32)
        for m in range(1, self.high):
            sent = lax.dynamic_index_in_dim(pieces, group ^ m, 0, False)
            total = total + self.flip(sent, self.far_bits[m]).astype(jnp.float32)
        return total


def add(one, two):
    return (one.astype(jnp.float32) + two.astype(jnp.float32)).astype(jnp.bfloat16)


def halve(groups, pieces, bit, place, axis):
    mine = place // bit % 2
    kept = lax.dynamic_index_in_dim(pieces, mine, axis, False).astype(jnp.float32)
    sent = groups.flip(lax.dynamic_index_in_dim(pieces, 1 - mine, axis, False), bit)
    return (kept + sent.astype(jnp.float32)).astype(jnp.bfloat16)


def stack_heads(flat, heads, upper):
    tall = jnp.concatenate([flat[:, h * HEAD : (h + 1) * HEAD] for h in range(heads)], axis=0)
    blank = jnp.zeros_like(tall)
    return jnp.concatenate([blank, tall] if upper else [tall, blank], axis=1)


def flat_heads(tall, heads):
    rows = tall.shape[0] // heads
    return jnp.concatenate([tall[h * rows : (h + 1) * rows] for h in range(heads)], axis=1)


def masked_scores(pair, wide, key_pos, query_pos):
    return jnp.where(key_pos <= query_pos, dot(pair, wide, 1, 1), MASKED)


def first_half(shape):
    return lax.broadcasted_iota(jnp.int32, shape, 1) % HEAD < HEAD // 2


def turn(values):
    width = values.shape[1]
    return jnp.where(
        first_half(values.shape),
        pltpu.roll(values, width - HEAD // 2, 1),
        pltpu.roll(values, HEAD // 2, 1),
    )


def widen(table, width):
    return jnp.concatenate([table] * (width // table.shape[1]), axis=1)


def project_kernel(
    heads, token_ref, w_ref, bias_ref, cosine_ref, sine_ref, normed_ref, query_ref, pair_ref
):
    normed, _ = norm_apply(token_ref[...].astype(jnp.float32))
    normed = normed.astype(jnp.bfloat16)
    normed_ref[...] = normed
    lin = dot(normed, w_ref[...], 1, 0) + bias_ref[...]
    width = (heads + 1) * HEAD
    some = lin[:, :width]
    turned = turn(some)
    turned = jnp.where(first_half(some.shape), -turned, turned)
    rotated = some * widen(cosine_ref[...], width) + turned * widen(sine_ref[...], width)
    rotated = rotated.astype(jnp.bfloat16)
    query_ref[...] = rotated[:, : heads * HEAD] * jnp.bfloat16(HEAD ** (-0.5))
    pair_ref[...] = jnp.concatenate(
        [rotated[:, heads * HEAD :], lin[:, width:].astype(jnp.bfloat16)], axis=1
    )


def whole_call(kernel, name, inputs, out_shape, scratch=(), place=None):
    whole = pl.BlockSpec(memory_space=pltpu.VMEM)
    in_specs = [whole] * len(inputs)
    if place is not None:
        inputs = (place.astype(jnp.int32)[None], *inputs)
        in_specs = [pl.BlockSpec(memory_space=pltpu.SMEM)] + in_specs
    return pl.pallas_call(
        kernel,
        in_specs=in_specs,
        out_specs=[whole] * len(out_shape),
        out_shape=out_shape,
        scratch_shapes=list(scratch),
        compiler_params=pltpu.CompilerParams(vmem_limit_bytes=VMEM_LIMIT),
        cost_estimate=BRIEF,
        name=name,
    )(*inputs)


def when(flag):
    if isinstance(flag, bool):
        return lambda body: body() if flag else None
    return pl.when(flag)


def forward_kernel(
    heads,
    steps,
    query_ref,
    pair_ref,
    key_pos_ref,
    query_pos_ref,
    w_out_ref,
    flat_ref,
    part_ref,
    out_ref,
    log_ref,
    best_ref,
    total_ref,
    sum_ref,
):
    step = 0 if steps == 1 else pl.program_id(1)
    for s in range(query_ref.shape[0]):

        @when(step == 0)
        def _():
            best_ref[s] = jnp.full(best_ref.shape[1:], LOWEST, jnp.float32)
            total_ref[s] = jnp.zeros(total_ref.shape[1:], jnp.float32)
            sum_ref[s] = jnp.zeros(sum_ref.shape[1:], jnp.float32)

        pair = pair_ref[:, s].reshape(-1, 2 * HEAD)
        wide = stack_heads(query_ref[s], heads, False)
        scores = masked_scores(pair, wide, key_pos_ref[s], query_pos_ref[s])
        best = best_ref[s]
        newest = jnp.maximum(best, jnp.max(scores, axis=0, keepdims=True))
        raised = jnp.exp(scores - newest)
        fading = jnp.exp(best - newest)
        best_ref[s] = newest
        total_ref[s] = total_ref[s] * fading + jnp.sum(raised, axis=0, keepdims=True)
        sum_ref[s] = sum_ref[s] * fading + dot(pair, raised.astype(jnp.bfloat16), 0, 0)

        @when(step == steps - 1)
        def _():
            out = sum_ref[s, HEAD:, :] / total_ref[s]
            if steps > 1:
                out_ref[s] = out
            log_ref[s] = best_ref[s] + jnp.log(total_ref[s])
            flat = flat_heads(out.T, heads).astype(jnp.bfloat16)
            flat_ref[s] = flat
            part_ref[s] = dot(flat, w_out_ref[...], 1, 1).astype(jnp.bfloat16)


def backward_kernel(
    heads,
    steps,
    query_ref,
    pair_ref,
    key_pos_ref,
    query_pos_ref,
    out_ref,
    log_ref,
    w_out_ref,
    own_ref,
    other_ref,
    hidden_ref,
    cotangent_ref,
    cosine_ref,
    sine_ref,
    d_hidden_ref,
    d_low_ref,
    d_query_ref,
    d_pair_ref,
    d_out_ref,
    dots_ref,
    sum_ref,
):
    step = 0 if steps == 1 else pl.program_id(1)
    for s in range(query_ref.shape[0]):

        @when(step == 0)
        def _():
            sum_ref[s] = jnp.zeros(sum_ref.shape[1:], jnp.float32)
            hidden = hidden_ref[s]
            weighted = own_ref[s].astype(jnp.float32) + other_ref[s].astype(jnp.float32)
            _, scale = norm_apply(hidden)
            d_hidden = cotangent_ref[s].astype(jnp.float32) + norm_back(hidden, scale, weighted)
            d_hidden_ref[s] = d_hidden
            low = d_hidden.astype(jnp.bfloat16)
            d_low_ref[s] = low
            flat = dot(low, w_out_ref[...], 1, 0).astype(jnp.bfloat16)
            d_out = stack_heads(flat, heads, True)
            d_out_ref[s] = d_out
            if steps > 1:
                dots_ref[s] = jnp.sum(
                    d_out[:, HEAD:].astype(jnp.float32).T * out_ref[s], axis=0, keepdims=True
                )

        pair = pair_ref[:, s].reshape(-1, 2 * HEAD)
        wide = stack_heads(query_ref[s], heads, False)
        d_out = d_out_ref[s]
        scores = masked_scores(pair, wide, key_pos_ref[s], query_pos_ref[s])
        chances = jnp.exp(scores - log_ref[s])
        d_chances = dot(pair, d_out, 1, 1)
        if steps > 1:
            dots = dots_ref[s]
        else:
            dots = jnp.sum(chances * d_chances, axis=0, keepdims=True)
        d_scores = (chances * (d_chances - dots)).astype(jnp.bfloat16)
        d_pair = dot(d_scores, wide, 1, 0) + dot(chances.astype(jnp.bfloat16), d_out, 1, 0)
        d_pair = d_pair.astype(jnp.bfloat16)
        d_pair_ref[:, s] = d_pair.reshape(d_pair_ref.shape[:1] + d_pair_ref.shape[2:])
        sum_ref[s] += dot(pair, d_scores, 0, 0)

        @when(step == steps - 1)
        def _():
            flat = flat_heads(sum_ref[s, :HEAD, :].T, heads) * (HEAD ** (-0.5))
            d_query_ref[s] = turn_back(flat, cosine_ref[s], sine_ref[s]).astype(jnp.bfloat16)


def turn_back(flat, cosine, sine):
    wide = -(-flat.shape[1] // 128) * 128
    blank = jnp.zeros((flat.shape[0], wide - flat.shape[1]), jnp.float32)
    padded = jnp.concatenate([flat, blank], axis=1) if wide > flat.shape[1] else flat
    turned = turn(padded * widen(sine, wide))
    turned = jnp.where(first_half(padded.shape), turned, -turned)
    return (padded * widen(cosine, wide) + turned)[:, : flat.shape[1]]


def attention_call(kernel, name, heads, rows, ctx, seqs, width, inputs, kinds, outs, scratch):
    group = min(ctx, 1024 // rows)
    steps = ctx // group
    span = group * rows
    tall = heads * rows
    wide = heads * HEAD
    shapes = {
        "flat": ((seqs, rows, wide), (1, rows, wide), lambda s, k: (s, 0, 0)),
        "model": ((seqs, rows, width), (1, rows, width), lambda s, k: (s, 0, 0)),
        "table": ((seqs, rows, 2 * HEAD), (1, rows, 2 * HEAD), lambda s, k: (s, 0, 0)),
        "pair": (
            (ctx, seqs, rows, 2 * HEAD),
            (group, 1, rows, 2 * HEAD),
            lambda s, k: (k, s, 0, 0),
        ),
        "key": ((seqs, ctx * rows, 1), (1, span, 1), lambda s, k: (s, k, 0)),
        "row": ((seqs, 1, tall), (1, 1, tall), lambda s, k: (s, 0, 0)),
        "out": ((seqs, HEAD, tall), (1, HEAD, tall), lambda s, k: (s, 0, 0)),
        "none": ((1, 8, 128), (1, 8, 128), lambda s, k: (0, 0, 0)),
        "weight": ((width, wide), (width, wide), lambda s, k: (0, 0)),
    }
    out_shape = [jax.ShapeDtypeStruct(shapes[kind][0], dtype) for kind, dtype in outs]
    here = seqs if steps == 1 else 1
    scratch = [pltpu.VMEM((here,) + shape, dtype) for shape, dtype in scratch]
    kernel = functools.partial(kernel, heads, steps)
    if steps == 1:
        return whole_call(kernel, name, inputs, out_shape, scratch)
    spec = lambda kind: pl.BlockSpec(shapes[kind][1], shapes[kind][2])
    return pl.pallas_call(
        kernel,
        grid=(seqs, steps),
        in_specs=[spec(kind) for kind in kinds],
        out_specs=[spec(kind) for kind, _ in outs],
        out_shape=out_shape,
        scratch_shapes=scratch,
        compiler_params=pltpu.CompilerParams(vmem_limit_bytes=VMEM_LIMIT),
        cost_estimate=BRIEF,
        name=name,
    )(*inputs)


def ffn_kernel(
    part,
    token_source,
    w_source,
    near_kept,
    near_sent,
    mixed_kept,
    mixed_sent,
    d_w_target,
    token_ref,
    w_ref,
    active_ref,
    d_gate_up_ref,
    grad_ref,
    model_ref,
    semaphores,
    sent_semaphores,
):
    models = (near_kept, near_sent, mixed_kept, mixed_sent)
    block = token_ref.shape[0] // 4
    gates = slice(0, 2 * part)
    downs = slice(2 * part, 3 * part)
    rows_of = lambda index: pl.ds(index * block, block)

    def load(source, target, index):
        copy = pltpu.make_async_copy(source, target, semaphores.at[index])
        copy.start()
        return copy

    copies = []

    def send(source, target):
        index = len(copies)
        copy = pltpu.make_async_copy(source, target, sent_semaphores.at[index])
        copy.start()
        copies.append(copy)

    def send_model(index, values):
        model_ref[index] = values.astype(jnp.bfloat16)
        send(model_ref.at[index], models[index])

    w_gates = load(w_source.at[:, gates], w_ref.at[:, gates], 4)
    tokens = {1: load(token_source.at[rows_of(1)], token_ref.at[rows_of(1)], 1)}
    tokens[3] = load(token_source.at[rows_of(3)], token_ref.at[rows_of(3)], 3)
    w_downs = load(w_source.at[:, downs], w_ref.at[:, downs], 5)
    for index in (0, 2):
        tokens[index] = load(token_source.at[rows_of(index)], token_ref.at[rows_of(index)], index)
    for half in (1, 0):
        rows = rows_of(half)
        tokens[half].wait()
        if half == 1:
            w_gates.wait()
        gate_up = dot(token_ref[rows, :], w_ref[:, gates], 1, 0)
        gate, up_values = gate_up[:, :part], gate_up[:, part:]
        sigma = 1.0 / (1.0 + jnp.exp(-gate))
        silu = gate * sigma
        active = (silu * up_values).astype(jnp.bfloat16)
        active_ref[rows, :] = active
        tokens[2 + half].wait()
        if half == 1:
            w_downs.wait()
        d_active = dot(token_ref[rows_of(2 + half), :], w_ref[:, downs], 1, 0)
        d_gate = d_active * up_values * sigma * (1.0 + gate * (1.0 - sigma))
        d_gate_up = jnp.concatenate([d_gate, d_active * silu], axis=1).astype(jnp.bfloat16)
        d_gate_up_ref[rows, :] = d_gate_up
        send_model(half, dot(d_gate_up, w_ref[:, gates], 1, 1))
        send_model(2 + half, dot(active, w_ref[:, downs], 1, 1))
    for index in range(3):
        columns = slice(index * part, (index + 1) * part)
        left = token_ref[: 2 * block, :] if index < 2 else token_ref[2 * block :, :]
        right = d_gate_up_ref[:, columns] if index < 2 else active_ref[...]
        grad_ref[:, columns] = dot(left, right, 0, 0).astype(jnp.bfloat16)
        send(grad_ref.at[:, columns], d_w_target.at[:, columns])
    for copy in copies:
        copy.wait()


def ffn_call(part, tokens, w_ffn):
    block, width = tokens.shape[0] // 4, tokens.shape[1]
    model = jax.ShapeDtypeStruct((block, width), jnp.bfloat16)
    far = pl.BlockSpec(memory_space=pltpu.HBM)
    return pl.pallas_call(
        functools.partial(ffn_kernel, part),
        in_specs=[far, far],
        out_specs=[far] * 5,
        out_shape=[model] * 4 + [jax.ShapeDtypeStruct(w_ffn.shape, jnp.bfloat16)],
        scratch_shapes=[
            pltpu.VMEM(tokens.shape, jnp.bfloat16),
            pltpu.VMEM(w_ffn.shape, jnp.bfloat16),
            pltpu.VMEM((2 * block, part), jnp.bfloat16),
            pltpu.VMEM((2 * block, 2 * part), jnp.bfloat16),
            pltpu.VMEM(w_ffn.shape, jnp.bfloat16),
            pltpu.VMEM((4, block, width), jnp.bfloat16),
            pltpu.SemaphoreType.DMA((6,)),
            pltpu.SemaphoreType.DMA((7,)),
        ],
        compiler_params=pltpu.CompilerParams(vmem_limit_bytes=FFN_VMEM_LIMIT),
        cost_estimate=BRIEF,
        name="ffn",
    )(tokens, w_ffn)


def split_rows(total, place_ref, share, kept_ref, sent_ref):
    odd = place_ref[0] % 2 == 1
    for index in range(total.shape[0] // (2 * share)):
        even_rows = total[2 * index * share : (2 * index + 1) * share]
        odd_rows = total[(2 * index + 1) * share : (2 * index + 2) * share]
        kept_ref[index] = jnp.where(odd, odd_rows, even_rows).astype(jnp.bfloat16)
        sent_ref[index] = jnp.where(odd, even_rows, odd_rows).astype(jnp.bfloat16)


def wide_kernel(share, place_ref, normed_ref, d_query_ref, d_low_ref, flat_ref, kept_ref, sent_ref):
    d_query = dot(normed_ref[...], d_query_ref[...], 0, 0)
    d_w_out = dot(d_low_ref[...], flat_ref[...], 0, 0)
    split_rows(jnp.concatenate([d_query, d_w_out], axis=1), place_ref, share, kept_ref, sent_ref)


def finish_kernel(
    share,
    place_ref,
    pair_ref,
    cosine_ref,
    sine_ref,
    normed_ref,
    token_ref,
    w_ref,
    d_query_ref,
    own_ref,
    other_ref,
    hidden_ref,
    same_ref,
    column_ref,
    weighted_ref,
    kept_ref,
    sent_ref,
):
    pair = pair_ref[...]
    turned = turn_back(pair, cosine_ref[...], sine_ref[...])
    lane = lax.broadcasted_iota(jnp.int32, pair.shape, 1)
    d_pair = jnp.where(lane < HEAD, turned, pair).astype(jnp.bfloat16)
    d_lin = jnp.concatenate([d_query_ref[...], d_pair], axis=1)
    weighted = dot(d_lin, w_ref[...], 1, 1)
    weighted_ref[...] = weighted.astype(jnp.bfloat16)
    count = pair.shape[0]
    d_pair_w = dot(normed_ref[...], d_pair, 0, 0)
    normed, _ = norm_apply(token_ref[...].astype(jnp.float32))
    hidden, _ = norm_apply(hidden_ref[...])
    weighted_two = own_ref[...].astype(jnp.float32) + other_ref[...].astype(jnp.float32)

    def spot(column):
        return (lax.broadcasted_iota(jnp.int32, (count, 128), 1) == column).astype(jnp.bfloat16)

    gains = dot((weighted * normed).astype(jnp.bfloat16), spot(0), 0, 0)
    gains = gains + dot((weighted_two * hidden).astype(jnp.bfloat16), spot(1), 0, 0)
    ones = jnp.ones((count, 128), jnp.bfloat16)
    bias = dot(d_lin, ones, 0, 0)
    bias = jnp.where(column_ref[...] > 0, bias, 0.0).astype(jnp.bfloat16)
    bias = dot(same_ref[...], bias, 1, 0)
    total = jnp.concatenate([d_pair_w, gains + bias], axis=1)
    split_rows(total, place_ref, share, kept_ref, sent_ref)


def local(
    tokens,
    cotangent,
    block_of,
    norm_gain,
    ffn_gain,
    w_query,
    w_key,
    w_value,
    b_query,
    b_key,
    b_value,
    w_out,
    w_gate,
    w_up,
    w_down,
):
    seqs, rows, width = tokens.shape
    count = seqs * rows
    block_len = rows // 2
    ctx = lax.axis_size("ctx")
    groups = Groups(ctx)
    low = groups.low
    device = lax.axis_index("ctx")
    heads = w_query.shape[1] // HEAD
    share = width // ctx
    units = w_gate.shape[1]
    part = -(-units // (low * 128)) * 128
    query_width = heads * HEAD
    own_gain_one = norm_gain.astype(jnp.float32)[:, None]
    own_gain_two = ffn_gain.astype(jnp.float32)[:, None]

    def scaled(matrix, gain):
        return (matrix.astype(jnp.float32) * gain).astype(jnp.bfloat16)

    def pieces(matrix):
        return jnp.pad(matrix, ((0, 0), (0, low * part - units))).reshape(share, low, part)

    w_ffn = jnp.concatenate(
        [
            pieces(scaled(w_gate, own_gain_two)),
            pieces(scaled(w_up, own_gain_two)),
            pieces(w_down.T),
        ],
        axis=2,
    ).transpose(1, 0, 2)
    w_attn = jnp.concatenate(
        [scaled(jnp.concatenate([w_query, w_key, w_value], axis=1), own_gain_one), w_out.T], axis=1
    )
    w_ffn, w_attn = together(w_ffn, w_attn)
    w_ffn = groups.swap_near(w_ffn).reshape(low * share, 3 * part)
    w_attn = groups.gather_far(w_attn, device)

    offsets = jnp.arange(block_len, dtype=jnp.int32)
    own_blocks = lax.dynamic_slice_in_dim(block_of, device * 2, 2, 1)
    row_pos = (own_blocks[:, :, None] * block_len + offsets).reshape(seqs, rows)
    query_pos = jnp.tile(row_pos, (1, heads))[:, None, :]
    flips = jnp.array(
        [core + step + far for core in (0, 1) for step in (0, 2) for far in groups.far_bits],
        jnp.int32,
    )
    key_blocks = block_of.reshape(seqs, ctx, 2)[:, device ^ flips]
    key_pos = (key_blocks[..., None] * block_len + offsets).reshape(seqs, ctx * rows, 1)
    cosine, sine = rope_tables(row_pos.reshape(count), HEAD)
    cosine, sine = jnp.tile(cosine, (1, 2)), jnp.tile(sine, (1, 2))

    qkv_width = query_width + 2 * HEAD
    row = jnp.arange(width)[:, None] % share
    unit = jnp.arange(qkv_width)[None, :]
    same = (row == unit % share).astype(jnp.bfloat16)
    column = (unit.T // share + 2 == jnp.arange(128)[None, :]).astype(jnp.float32)
    w_ffn, w_attn, key_pos, query_pos, cosine, sine, same, column = together(
        w_ffn, w_attn, key_pos, query_pos, cosine, sine, same, column
    )
    w_ffn = lax.all_gather(w_ffn, "ctx", axis=0, tiled=True, axis_index_groups=groups.far)
    w_qkv = groups.spread_near(w_attn[:, :, :qkv_width])
    grads_in = cotangent.reshape(count, width)

    bias = jnp.concatenate([b_query, b_key, b_value]).astype(jnp.float32)[None]
    normed_low, queries, pair = whole_call(
        functools.partial(project_kernel, heads),
        "project",
        (tokens.reshape(count, width), w_qkv, bias, cosine, sine),
        [
            jax.ShapeDtypeStruct((count, width), jnp.bfloat16),
            jax.ShapeDtypeStruct((count, query_width), jnp.bfloat16),
            jax.ShapeDtypeStruct((count, 2 * HEAD), jnp.bfloat16),
        ],
    )
    queries = queries.reshape(seqs, rows, query_width)
    pairs = groups.far_flips(pair)
    w_out_t = groups.flip_near(w_attn[:, :, qkv_width:], device)
    pairs = jnp.stack([pairs, groups.flip(pairs, 2)])
    pairs = jnp.stack([pairs, groups.flip(pairs, 1)]).reshape(ctx, seqs, rows, 2 * HEAD)
    pairs, w_out_t = together(pairs, w_out_t)
    attend = functools.partial(
        attention_call, heads=heads, rows=rows, ctx=ctx, seqs=seqs, width=width
    )
    tall = heads * rows
    tall_kind = "out" if ctx * rows > 1024 else "none"
    out_flat, attention, out_tall, log_total = attend(
        forward_kernel,
        "forward",
        inputs=(queries, pairs, key_pos, query_pos, w_out_t),
        kinds=("flat", "pair", "key", "row", "weight"),
        outs=(
            ("flat", jnp.bfloat16),
            ("model", jnp.bfloat16),
            (tall_kind, jnp.float32),
            ("row", jnp.float32),
        ),
        scratch=[
            ((1, tall), jnp.float32),
            ((1, tall), jnp.float32),
            ((2 * HEAD, tall), jnp.float32),
        ],
    )
    out_flat = out_flat.reshape(count, query_width)
    inputs = tokens.astype(jnp.float32).reshape(count, width)
    hidden = inputs + sum_tp(attention.reshape(count, width))

    grads_near = groups.gather_near(grads_in)
    hidden, *grads_near = together(hidden, *grads_near)
    normed_two, _ = norm_apply(hidden)
    near_two = groups.gather_near(normed_two.astype(jnp.bfloat16))
    token_parts = jnp.concatenate([*near_two, *grads_near], axis=0)
    near_kept, near_sent, mixed_kept, mixed_sent, d_w_ffn = ffn_call(part, token_parts, w_ffn)
    d_w_ffn = lax.psum_scatter(
        d_w_ffn, "ctx", scatter_dimension=0, tiled=True, axis_index_groups=groups.far
    )
    crossed = groups.flip(near_sent, 1)
    near_sent = groups.flip(add(near_kept[count:], crossed[count:]), 2)
    d_own = add(add(near_kept[:count], crossed[:count]), near_sent)
    mixed_sent = groups.flip(mixed_sent, 1)
    d_own, mixed_sent = together(d_own, mixed_sent)
    d_other = lax.ppermute(d_own, "tp", [(0, 1), (1, 0)])
    mixed_kept = add(mixed_kept, mixed_sent)
    d_other, mixed_kept = together(d_other, mixed_kept)
    mixed_own = add(mixed_kept[:count], groups.flip(mixed_kept[count:], 2))

    by_seq = lambda values: values.reshape((seqs, rows) + values.shape[1:])
    d_hidden, d_hidden_low, d_query_low, d_pairs = attend(
        backward_kernel,
        "backward",
        inputs=(
            queries,
            pairs,
            key_pos,
            query_pos,
            out_tall,
            log_total,
            w_out_t,
            by_seq(d_own),
            by_seq(d_other),
            by_seq(hidden),
            cotangent,
            by_seq(cosine),
            by_seq(sine),
        ),
        kinds=(
            ("flat", "pair", "key", "row", tall_kind, "row", "weight")
            + ("model", "model", "model", "model", "table", "table")
        ),
        outs=(
            ("model", jnp.float32),
            ("model", jnp.bfloat16),
            ("flat", jnp.bfloat16),
            ("pair", jnp.bfloat16),
        ),
        scratch=[
            ((tall, 2 * HEAD), jnp.bfloat16),
            ((1, tall), jnp.float32),
            ((2 * HEAD, tall), jnp.float32),
        ],
    )
    d_hidden = d_hidden.reshape(count, width)
    d_hidden_low = d_hidden_low.reshape(count, width)
    d_query_low = d_query_low.reshape(count, query_width)
    d_pairs, mixed_own = together(d_pairs, mixed_own)
    mixed_other = lax.ppermute(mixed_own, "tp", [(0, 1), (1, 0)])
    d_pairs = d_pairs.reshape(2, 2 * groups.high * count, 2 * HEAD)
    crossed = groups.flip(d_pairs[1], 1)
    crossed, d_query_low = together(crossed, d_query_low)
    halves = lambda columns: [jax.ShapeDtypeStruct((ctx // 2, share, columns), jnp.bfloat16)] * 2
    wide_kept, wide_sent = whole_call(
        functools.partial(wide_kernel, share),
        "wide",
        (normed_low, d_query_low, d_hidden_low, out_flat),
        halves(2 * query_width),
        place=device,
    )
    wide_crossed = groups.flip(wide_sent, 1)
    d_pairs = add(d_pairs[0], crossed).reshape(2, groups.high * count, 2 * HEAD)
    d_pairs = add(d_pairs[0], groups.flip(d_pairs[1], 2)).reshape(groups.high, count, 2 * HEAD)
    d_pairs, wide_crossed = together(d_pairs, wide_crossed)

    def near_half(kept, crossed):
        pieces = add(kept, crossed).reshape((groups.high, 2) + kept.shape[1:])
        mine = device // 2 % 2
        sent = lax.dynamic_index_in_dim(pieces, 1 - mine, 1, False)
        return lax.dynamic_index_in_dim(pieces, mine, 1, False), groups.flip(sent, 2)

    wide_kept, wide_beside = near_half(wide_kept, wide_crossed)
    pair_grads = d_pairs[0].astype(jnp.float32)
    for m in range(1, groups.high):
        pair_grads = pair_grads + groups.flip(d_pairs[m], groups.far_bits[m]).astype(jnp.float32)
    pair_grads, wide_beside = together(pair_grads, wide_beside)
    mixed = hidden + mixed_own.astype(jnp.float32) + mixed_other.astype(jnp.float32)
    mixed = mixed.astype(jnp.bfloat16)

    d_weighted_low, narrow_kept, narrow_sent = whole_call(
        functools.partial(finish_kernel, share),
        "finish",
        (
            pair_grads,
            cosine,
            sine,
            normed_low,
            tokens.reshape(count, width),
            w_qkv,
            d_query_low,
            d_own,
            d_other,
            hidden,
            same,
            column,
        ),
        [
            jax.ShapeDtypeStruct((count, width), jnp.bfloat16),
            *halves(256),
        ],
        place=device,
    )
    narrow_kept, narrow_beside = near_half(narrow_kept, groups.flip(narrow_sent, 1))
    narrow = add(narrow_kept, narrow_beside)
    extra = narrow[:, :, 2 * HEAD :]
    other = lax.ppermute(extra, "tp", [(0, 1), (1, 0)])
    first = lax.broadcasted_iota(jnp.int32, extra.shape, 2) == 0
    extra = jnp.where(first, add(extra, other), extra)
    narrow = jnp.concatenate(
        [add(wide_kept, wide_beside), narrow[:, :, : 2 * HEAD], extra], axis=2
    )
    narrow, d_w_ffn, d_weighted_low, mixed = together(narrow, d_w_ffn, d_weighted_low, mixed)
    d_weighted = sum_tp(d_weighted_low)
    _, scale_one = norm_apply(inputs)
    tokens_grad = (d_hidden + norm_back(inputs, scale_one, d_weighted)).astype(jnp.bfloat16)
    d_w_ffn = groups.swap_near(d_w_ffn.reshape(low, share, 3 * part))
    narrow = groups.far_owner(narrow, device)
    d_w_wide, narrow = narrow[:, : 2 * query_width], narrow[:, 2 * query_width :]

    def whole(swapped, index):
        some = swapped[:, :, index * part : (index + 1) * part].transpose(1, 0, 2)
        return some.reshape(share, low * part)[:, :units].astype(jnp.float32)

    g_gate = whole(d_w_ffn, 0) * own_gain_two
    g_up = whole(d_w_ffn, 1) * own_gain_two
    g_down = whole(d_w_ffn, 2).T

    held = -(-qkv_width // share)
    g_bias = narrow[:, 2 * HEAD + 2 : 2 * HEAD + 2 + held].T.reshape(held * share)
    g_pair = narrow[:, : 2 * HEAD] * own_gain_one
    g_two = narrow[:, 2 * HEAD + 1] / own_gain_two[:, 0]
    g_one = narrow[:, 2 * HEAD] / own_gain_one[:, 0]
    return (
        mixed.reshape(tokens.shape),
        tokens_grad.reshape(tokens.shape),
        g_one,
        g_two,
        d_w_wide[:, :query_width] * own_gain_one,
        g_pair[:, :HEAD],
        g_pair[:, HEAD:],
        g_bias[:query_width],
        g_bias[query_width : query_width + HEAD],
        g_bias[query_width + HEAD : query_width + 2 * HEAD],
        d_w_wide[:, query_width:].T,
        g_gate,
        g_up,
        g_down,
    )


def solution(mesh):
    placed = (
        P(None, "ctx", None),
        P(None, "ctx", None),
        P(),
        P("ctx"),
        P("ctx"),
        P("ctx", "tp"),
        P("ctx", "tp"),
        P("ctx", "tp"),
        P("tp"),
        P("tp"),
        P("tp"),
        P("tp", "ctx"),
        P("ctx", "tp"),
        P("ctx", "tp"),
        P("tp", "ctx"),
    )
    return jax.shard_map(
        local,
        mesh=mesh,
        in_specs=placed,
        out_specs=(
            P(None, "ctx", None),
            P(None, "ctx", None),
            P("ctx"),
            P("ctx"),
            P("ctx", "tp"),
            P("ctx", "tp"),
            P("ctx", "tp"),
            P("tp"),
            P("tp"),
            P("tp"),
            P("tp", "ctx"),
            P("ctx", "tp"),
            P("ctx", "tp"),
            P("tp", "ctx"),
        ),
        check_vma=False,
    )
```

```python
import functools

import jax
import jax.numpy as jnp
from jax import lax
from jax.experimental import pallas as pl
from jax.experimental.pallas import tpu as pltpu
from jax.sharding import PartitionSpec as P

HEAD = 64


EPSILON = 1e-06
ROPE_BASE = 1000000.0
MASKED = -1e30
LOWEST = -1e29
BRIEF = pl.CostEstimate(flops=1, bytes_accessed=1, transcendentals=0)
VMEM_LIMIT = 32 * 1024 * 1024
FFN_VMEM_LIMIT = 56 * 1024 * 1024


def rope_tables(positions, head_dim):
    halfway = head_dim // 2
    inverse = ROPE_BASE ** (-(jnp.arange(halfway, dtype=jnp.float32) * 2.0 / head_dim))
    angles = positions.astype(jnp.float32)[..., None] * inverse
    angles = jnp.concatenate([angles, angles], axis=-1)
    return (jnp.cos(angles), jnp.sin(angles))


def norm_apply(values):
    factor = lax.rsqrt(jnp.mean(values * values, axis=-1, keepdims=True) + EPSILON)
    return values * factor, factor


def norm_back(values, factor, weighted):
    inner = jnp.mean(weighted * values, axis=-1, keepdims=True)
    return factor * weighted - values * factor * factor * factor * inner


def dot(left, right, left_dim, right_dim):
    return lax.dot_general(
        left, right, (((left_dim,), (right_dim,)), ((), ())), preferred_element_type=jnp.float32
    )


def sum_tp(values):
    other = lax.ppermute(values, "tp", [(0, 1), (1, 0)])
    return values.astype(jnp.float32) + other.astype(jnp.float32)


def together(*values):
    return lax.optimization_barrier(values)


class Groups:
    def __init__(self, count):
        self.count = count
        self.low = 4
        self.high = count // self.low
        self.near = [[base + here for here in range(4)] for base in range(0, count, 4)]
        self.far = [list(group) for group in zip(*self.near)]
        self.far_bits = list(range(0, count, 4))

    def flip(self, values, bit):
        return lax.ppermute(values, "ctx", [(i, i ^ bit) for i in range(self.count)])

    def swap_near(self, values):
        return lax.all_to_all(values, "ctx", 0, 0, tiled=True, axis_index_groups=self.near)

    def gather_near(self, values):
        first = jnp.concatenate([values, self.flip(values, 2)], axis=0)
        return first, self.flip(first, 1)

    def far_flips(self, values):
        return jnp.stack([values] + [self.flip(values, bits) for bits in self.far_bits[1:]])


    def gather_far(self, values, place):
        if self.high != 4:
            return lax.all_gather(values, "ctx", axis=0, axis_index_groups=self.far)
        far = self.far_flips(values).reshape((2, 2) + values.shape)
        far = jnp.where(place // 8 % 2 == 1, far[::-1], far)
        far = jnp.where(place // 4 % 2 == 1, far[:, ::-1], far)
        return far.reshape((4,) + values.shape)

    def spread_near(self, values):
        whole = lax.all_gather(values, "ctx", axis=0, axis_index_groups=self.near)
        whole = jnp.swapaxes(whole, 0, 1)
        return whole.reshape((self.count * values.shape[1],) + values.shape[2:])

    def flip_near(self, values, place):
        other = self.flip(values, 2)
        upper = place // 2 % 2 == 1
        both = jnp.stack([jnp.where(upper, other, values), jnp.where(upper, values, other)], axis=1)
        other = self.flip(both, 1)
        upper = place % 2 == 1
        whole = jnp.stack([jnp.where(upper, other, both), jnp.where(upper, both, other)], axis=2)
        return whole.reshape((self.count * values.shape[1],) + values.shape[2:])

    def far_owner(self, pieces, place):
        if self.high != 4:
            shape = pieces.shape
            pieces = pieces.reshape((shape[0] * shape[1],) + shape[2:])
            return lax.psum_scatter(
                pieces, "ctx", scatter_dimension=0, tiled=True, axis_index_groups=self.far
            ).astype(jnp.float32)
        group = place // self.low
        total = lax.dynamic_index_in_dim(pieces, group, 0, False).astype(jnp.float32)
        for m in range(1, self.high):
            sent = lax.dynamic_index_in_dim(pieces, group ^ m, 0, False)
            total = total + self.flip(sent, self.far_bits[m]).astype(jnp.float32)
        return total


def add(one, two):
    return (one.astype(jnp.float32) + two.astype(jnp.float32)).astype(jnp.bfloat16)


def halve(groups, pieces, bit, place, axis):
    mine = place // bit % 2
    kept = lax.dynamic_index_in_dim(pieces, mine, axis, False).astype(jnp.float32)
    sent = groups.flip(lax.dynamic_index_in_dim(pieces, 1 - mine, axis, False), bit)
    return (kept + sent.astype(jnp.float32)).astype(jnp.bfloat16)


def stack_heads(flat, heads, upper):
    tall = jnp.concatenate([flat[:, h * HEAD : (h + 1) * HEAD] for h in range(heads)], axis=0)
    blank = jnp.zeros_like(tall)
    return jnp.concatenate([blank, tall] if upper else [tall, blank], axis=1)


def flat_heads(tall, heads):
    rows = tall.shape[0] // heads
    return jnp.concatenate([tall[h * rows : (h + 1) * rows] for h in range(heads)], axis=1)


def masked_scores(pair, wide, key_pos, query_pos):
    return jnp.where(key_pos <= query_pos, dot(pair, wide, 1, 1), MASKED)


def first_half(shape):
    return lax.broadcasted_iota(jnp.int32, shape, 1) % HEAD < HEAD // 2


def turn(values):
    width = values.shape[1]
    return jnp.where(
        first_half(values.shape),
        pltpu.roll(values, width - HEAD // 2, 1),
        pltpu.roll(values, HEAD // 2, 1),
    )


def widen(table, width):
    return jnp.concatenate([table] * (width // table.shape[1]), axis=1)


def project_kernel(
    heads, token_ref, w_ref, bias_ref, cosine_ref, sine_ref, normed_ref, query_ref, pair_ref
):
    normed, _ = norm_apply(token_ref[...].astype(jnp.float32))
    normed = normed.astype(jnp.bfloat16)
    normed_ref[...] = normed
    lin = dot(normed, w_ref[...], 1, 0) + bias_ref[...]
    width = (heads + 1) * HEAD
    some = lin[:, :width]
    turned = turn(some)
    turned = jnp.where(first_half(some.shape), -turned, turned)
    rotated = some * widen(cosine_ref[...], width) + turned * widen(sine_ref[...], width)
    rotated = rotated.astype(jnp.bfloat16)
    query_ref[...] = rotated[:, : heads * HEAD] * jnp.bfloat16(HEAD ** (-0.5))
    pair_ref[...] = jnp.concatenate(
        [rotated[:, heads * HEAD :], lin[:, width:].astype(jnp.bfloat16)], axis=1
    )


def whole_call(kernel, name, inputs, out_shape, scratch=(), place=None):
    whole = pl.BlockSpec(memory_space=pltpu.VMEM)
    in_specs = [whole] * len(inputs)
    if place is not None:
        inputs = (place.astype(jnp.int32)[None], *inputs)
        in_specs = [pl.BlockSpec(memory_space=pltpu.SMEM)] + in_specs
    return pl.pallas_call(
        kernel,
        in_specs=in_specs,
        out_specs=[whole] * len(out_shape),
        out_shape=out_shape,
        scratch_shapes=list(scratch),
        compiler_params=pltpu.CompilerParams(vmem_limit_bytes=VMEM_LIMIT),
        cost_estimate=BRIEF,
        name=name,
    )(*inputs)


def when(flag):
    if isinstance(flag, bool):
        return lambda body: body() if flag else None
    return pl.when(flag)


def forward_kernel(
    heads,
    steps,
    query_ref,
    pair_ref,
    key_pos_ref,
    query_pos_ref,
    w_out_ref,
    flat_ref,
    part_ref,
    out_ref,
    log_ref,
    best_ref,
    total_ref,
    sum_ref,
):
    step = 0 if steps == 1 else pl.program_id(1)
    for s in range(query_ref.shape[0]):

        @when(step == 0)
        def _():
            best_ref[s] = jnp.full(best_ref.shape[1:], LOWEST, jnp.float32)
            total_ref[s] = jnp.zeros(total_ref.shape[1:], jnp.float32)
            sum_ref[s] = jnp.zeros(sum_ref.shape[1:], jnp.float32)

        pair = pair_ref[:, s].reshape(-1, 2 * HEAD)
        wide = stack_heads(query_ref[s], heads, False)
        scores = masked_scores(pair, wide, key_pos_ref[s], query_pos_ref[s])
        best = best_ref[s]
        newest = jnp.maximum(best, jnp.max(scores, axis=0, keepdims=True))
        raised = jnp.exp(scores - newest)
        fading = jnp.exp(best - newest)
        best_ref[s] = newest
        total_ref[s] = total_ref[s] * fading + jnp.sum(raised, axis=0, keepdims=True)
        sum_ref[s] = sum_ref[s] * fading + dot(pair, raised.astype(jnp.bfloat16), 0, 0)

        @when(step == steps - 1)
        def _():
            out = sum_ref[s, HEAD:, :] / total_ref[s]
            if steps > 1:
                out_ref[s] = out
            log_ref[s] = best_ref[s] + jnp.log(total_ref[s])
            flat = flat_heads(out.T, heads).astype(jnp.bfloat16)
            flat_ref[s] = flat
            part_ref[s] = dot(flat, w_out_ref[...], 1, 1).astype(jnp.bfloat16)


def backward_kernel(
    heads,
    steps,
    query_ref,
    pair_ref,
    key_pos_ref,
    query_pos_ref,
    out_ref,
    log_ref,
    w_out_ref,
    own_ref,
    other_ref,
    hidden_ref,
    cotangent_ref,
    cosine_ref,
    sine_ref,
    d_hidden_ref,
    d_low_ref,
    d_query_ref,
    d_pair_ref,
    d_out_ref,
    dots_ref,
    sum_ref,
):
    step = 0 if steps == 1 else pl.program_id(1)
    for s in range(query_ref.shape[0]):

        @when(step == 0)
        def _():
            sum_ref[s] = jnp.zeros(sum_ref.shape[1:], jnp.float32)
            hidden = hidden_ref[s]
            weighted = own_ref[s].astype(jnp.float32) + other_ref[s].astype(jnp.float32)
            _, scale = norm_apply(hidden)
            d_hidden = cotangent_ref[s].astype(jnp.float32) + norm_back(hidden, scale, weighted)
            d_hidden_ref[s] = d_hidden
            low = d_hidden.astype(jnp.bfloat16)
            d_low_ref[s] = low
            flat = dot(low, w_out_ref[...], 1, 0).astype(jnp.bfloat16)
            d_out = stack_heads(flat, heads, True)
            d_out_ref[s] = d_out
            if steps > 1:
                dots_ref[s] = jnp.sum(
                    d_out[:, HEAD:].astype(jnp.float32).T * out_ref[s], axis=0, keepdims=True
                )

        pair = pair_ref[:, s].reshape(-1, 2 * HEAD)
        wide = stack_heads(query_ref[s], heads, False)
        d_out = d_out_ref[s]
        scores = masked_scores(pair, wide, key_pos_ref[s], query_pos_ref[s])
        chances = jnp.exp(scores - log_ref[s])
        d_chances = dot(pair, d_out, 1, 1)
        if steps > 1:
            dots = dots_ref[s]
        else:
            dots = jnp.sum(chances * d_chances, axis=0, keepdims=True)
        d_scores = (chances * (d_chances - dots)).astype(jnp.bfloat16)
        d_pair = dot(d_scores, wide, 1, 0) + dot(chances.astype(jnp.bfloat16), d_out, 1, 0)
        d_pair = d_pair.astype(jnp.bfloat16)
        d_pair_ref[:, s] = d_pair.reshape(d_pair_ref.shape[:1] + d_pair_ref.shape[2:])
        sum_ref[s] += dot(pair, d_scores, 0, 0)

        @when(step == steps - 1)
        def _():
            flat = flat_heads(sum_ref[s, :HEAD, :].T, heads) * (HEAD ** (-0.5))
            d_query_ref[s] = turn_back(flat, cosine_ref[s], sine_ref[s]).astype(jnp.bfloat16)


def turn_back(flat, cosine, sine):
    wide = -(-flat.shape[1] // 128) * 128
    blank = jnp.zeros((flat.shape[0], wide - flat.shape[1]), jnp.float32)
    padded = jnp.concatenate([flat, blank], axis=1) if wide > flat.shape[1] else flat
    turned = turn(padded * widen(sine, wide))
    turned = jnp.where(first_half(padded.shape), turned, -turned)
    return (padded * widen(cosine, wide) + turned)[:, : flat.shape[1]]


def attention_call(kernel, name, heads, rows, ctx, seqs, width, inputs, kinds, outs, scratch):
    group = min(ctx, 1024 // rows)
    steps = ctx // group
    span = group * rows
    tall = heads * rows
    wide = heads * HEAD
    shapes = {
        "flat": ((seqs, rows, wide), (1, rows, wide), lambda s, k: (s, 0, 0)),
        "model": ((seqs, rows, width), (1, rows, width), lambda s, k: (s, 0, 0)),
        "table": ((seqs, rows, 2 * HEAD), (1, rows, 2 * HEAD), lambda s, k: (s, 0, 0)),
        "pair": (
            (ctx, seqs, rows, 2 * HEAD),
            (group, 1, rows, 2 * HEAD),
            lambda s, k: (k, s, 0, 0),
        ),
        "key": ((seqs, ctx * rows, 1), (1, span, 1), lambda s, k: (s, k, 0)),
        "row": ((seqs, 1, tall), (1, 1, tall), lambda s, k: (s, 0, 0)),
        "out": ((seqs, HEAD, tall), (1, HEAD, tall), lambda s, k: (s, 0, 0)),
        "none": ((1, 8, 128), (1, 8, 128), lambda s, k: (0, 0, 0)),
        "weight": ((width, wide), (width, wide), lambda s, k: (0, 0)),
    }
    out_shape = [jax.ShapeDtypeStruct(shapes[kind][0], dtype) for kind, dtype in outs]
    here = seqs if steps == 1 else 1
    scratch = [pltpu.VMEM((here,) + shape, dtype) for shape, dtype in scratch]
    kernel = functools.partial(kernel, heads, steps)
    if steps == 1:
        return whole_call(kernel, name, inputs, out_shape, scratch)
    spec = lambda kind: pl.BlockSpec(shapes[kind][1], shapes[kind][2])
    return pl.pallas_call(
        kernel,
        grid=(seqs, steps),
        in_specs=[spec(kind) for kind in kinds],
        out_specs=[spec(kind) for kind, _ in outs],
        out_shape=out_shape,
        scratch_shapes=scratch,
        compiler_params=pltpu.CompilerParams(vmem_limit_bytes=VMEM_LIMIT),
        cost_estimate=BRIEF,
        name=name,
    )(*inputs)


def ffn_kernel(
    part,
    token_source,
    w_source,
    near_kept,
    near_sent,
    mixed_kept,
    mixed_sent,
    d_w_target,
    token_ref,
    w_ref,
    active_ref,
    d_gate_up_ref,
    grad_ref,
    model_ref,
    semaphores,
    sent_semaphores,
):
    models = (near_kept, near_sent, mixed_kept, mixed_sent)
    block = token_ref.shape[0] // 4
    gates = slice(0, 2 * part)
    downs = slice(2 * part, 3 * part)
    rows_of = lambda index: pl.ds(index * block, block)

    def load(source, target, index):
        copy = pltpu.make_async_copy(source, target, semaphores.at[index])
        copy.start()
        return copy

    copies = []

    def send(source, target):
        index = len(copies)
        copy = pltpu.make_async_copy(source, target, sent_semaphores.at[index])
        copy.start()
        copies.append(copy)

    def send_model(index, values):
        model_ref[index] = values.astype(jnp.bfloat16)
        send(model_ref.at[index], models[index])

    w_gates = load(w_source.at[:, gates], w_ref.at[:, gates], 4)
    tokens = {1: load(token_source.at[rows_of(1)], token_ref.at[rows_of(1)], 1)}
    tokens[3] = load(token_source.at[rows_of(3)], token_ref.at[rows_of(3)], 3)
    w_downs = load(w_source.at[:, downs], w_ref.at[:, downs], 5)
    for index in (0, 2):
        tokens[index] = load(token_source.at[rows_of(index)], token_ref.at[rows_of(index)], index)
    for half in (1, 0):
        rows = rows_of(half)
        tokens[half].wait()
        if half == 1:
            w_gates.wait()
        gate_up = dot(token_ref[rows, :], w_ref[:, gates], 1, 0)
        gate, up_values = gate_up[:, :part], gate_up[:, part:]
        sigma = 1.0 / (1.0 + jnp.exp(-gate))
        silu = gate * sigma
        active = (silu * up_values).astype(jnp.bfloat16)
        active_ref[rows, :] = active
        tokens[2 + half].wait()
        if half == 1:
            w_downs.wait()
        d_active = dot(token_ref[rows_of(2 + half), :], w_ref[:, downs], 1, 0)
        d_gate = d_active * up_values * sigma * (1.0 + gate * (1.0 - sigma))
        d_gate_up = jnp.concatenate([d_gate, d_active * silu], axis=1).astype(jnp.bfloat16)
        d_gate_up_ref[rows, :] = d_gate_up
        send_model(half, dot(d_gate_up, w_ref[:, gates], 1, 1))
        send_model(2 + half, dot(active, w_ref[:, downs], 1, 1))
    for index in range(3):
        columns = slice(index * part, (index + 1) * part)
        left = token_ref[: 2 * block, :] if index < 2 else token_ref[2 * block :, :]
        right = d_gate_up_ref[:, columns] if index < 2 else active_ref[...]
        grad_ref[:, columns] = dot(left, right, 0, 0).astype(jnp.bfloat16)
        send(grad_ref.at[:, columns], d_w_target.at[:, columns])
    for copy in copies:
        copy.wait()


def ffn_call(part, tokens, w_ffn):
    block, width = tokens.shape[0] // 4, tokens.shape[1]
    model = jax.ShapeDtypeStruct((block, width), jnp.bfloat16)
    far = pl.BlockSpec(memory_space=pltpu.HBM)
    return pl.pallas_call(
        functools.partial(ffn_kernel, part),
        in_specs=[far, far],
        out_specs=[far] * 5,
        out_shape=[model] * 4 + [jax.ShapeDtypeStruct(w_ffn.shape, jnp.bfloat16)],
        scratch_shapes=[
            pltpu.VMEM(tokens.shape, jnp.bfloat16),
            pltpu.VMEM(w_ffn.shape, jnp.bfloat16),
            pltpu.VMEM((2 * block, part), jnp.bfloat16),
            pltpu.VMEM((2 * block, 2 * part), jnp.bfloat16),
            pltpu.VMEM(w_ffn.shape, jnp.bfloat16),
            pltpu.VMEM((4, block, width), jnp.bfloat16),
            pltpu.SemaphoreType.DMA((6,)),
            pltpu.SemaphoreType.DMA((7,)),
        ],
        compiler_params=pltpu.CompilerParams(vmem_limit_bytes=FFN_VMEM_LIMIT),
        cost_estimate=BRIEF,
        name="ffn",
    )(tokens, w_ffn)


def split_rows(total, place_ref, share, kept_ref, sent_ref):
    odd = place_ref[0] % 2 == 1
    for index in range(total.shape[0] // (2 * share)):
        even_rows = total[2 * index * share : (2 * index + 1) * share]
        odd_rows = total[(2 * index + 1) * share : (2 * index + 2) * share]
        kept_ref[index] = jnp.where(odd, odd_rows, even_rows).astype(jnp.bfloat16)
        sent_ref[index] = jnp.where(odd, even_rows, odd_rows).astype(jnp.bfloat16)


def wide_kernel(share, place_ref, normed_ref, d_query_ref, d_low_ref, flat_ref, kept_ref, sent_ref):
    d_query = dot(normed_ref[...], d_query_ref[...], 0, 0)
    d_w_out = dot(d_low_ref[...], flat_ref[...], 0, 0)
    split_rows(jnp.concatenate([d_query, d_w_out], axis=1), place_ref, share, kept_ref, sent_ref)


def finish_kernel(
    share,
    place_ref,
    pair_ref,
    cosine_ref,
    sine_ref,
    normed_ref,
    token_ref,
    w_ref,
    d_query_ref,
    own_ref,
    other_ref,
    hidden_ref,
    same_ref,
    column_ref,
    weighted_ref,
    kept_ref,
    sent_ref,
):
    pair = pair_ref[...]
    turned = turn_back(pair, cosine_ref[...], sine_ref[...])
    lane = lax.broadcasted_iota(jnp.int32, pair.shape, 1)
    d_pair = jnp.where(lane < HEAD, turned, pair).astype(jnp.bfloat16)
    d_lin = jnp.concatenate([d_query_ref[...], d_pair], axis=1)
    weighted = dot(d_lin, w_ref[...], 1, 1)
    weighted_ref[...] = weighted.astype(jnp.bfloat16)
    count = pair.shape[0]
    d_pair_w = dot(normed_ref[...], d_pair, 0, 0)
    normed, _ = norm_apply(token_ref[...].astype(jnp.float32))
    hidden, _ = norm_apply(hidden_ref[...])
    weighted_two = own_ref[...].astype(jnp.float32) + other_ref[...].astype(jnp.float32)

    def spot(column):
        return (lax.broadcasted_iota(jnp.int32, (count, 128), 1) == column).astype(jnp.bfloat16)

    gains = dot((weighted * normed).astype(jnp.bfloat16), spot(0), 0, 0)
    gains = gains + dot((weighted_two * hidden).astype(jnp.bfloat16), spot(1), 0, 0)
    ones = jnp.ones((count, 128), jnp.bfloat16)
    bias = dot(d_lin, ones, 0, 0)
    bias = jnp.where(column_ref[...] > 0, bias, 0.0).astype(jnp.bfloat16)
    bias = dot(same_ref[...], bias, 1, 0)
    total = jnp.concatenate([d_pair_w, gains + bias], axis=1)
    split_rows(total, place_ref, share, kept_ref, sent_ref)


def local(
    tokens,
    cotangent,
    block_of,
    norm_gain,
    ffn_gain,
    w_query,
    w_key,
    w_value,
    b_query,
    b_key,
    b_value,
    w_out,
    w_gate,
    w_up,
    w_down,
):
    seqs, rows, width = tokens.shape
    count = seqs * rows
    block_len = rows // 2
    ctx = lax.axis_size("ctx")
    groups = Groups(ctx)
    low = groups.low
    device = lax.axis_index("ctx")
    heads = w_query.shape[1] // HEAD
    share = width // ctx
    units = w_gate.shape[1]
    part = -(-units // (low * 128)) * 128
    query_width = heads * HEAD
    own_gain_one = norm_gain.astype(jnp.float32)[:, None]
    own_gain_two = ffn_gain.astype(jnp.float32)[:, None]

    def scaled(matrix, gain):
        return (matrix.astype(jnp.float32) * gain).astype(jnp.bfloat16)

    def pieces(matrix):
        return jnp.pad(matrix, ((0, 0), (0, low * part - units))).reshape(share, low, part)

    w_ffn = jnp.concatenate(
        [
            pieces(scaled(w_gate, own_gain_two)),
            pieces(scaled(w_up, own_gain_two)),
            pieces(w_down.T),
        ],
        axis=2,
    ).transpose(1, 0, 2)
    w_attn = jnp.concatenate(
        [scaled(jnp.concatenate([w_query, w_key, w_value], axis=1), own_gain_one), w_out.T], axis=1
    )
    w_ffn, w_attn = together(w_ffn, w_attn)
    w_ffn = groups.swap_near(w_ffn).reshape(low * share, 3 * part)
    w_attn = groups.gather_far(w_attn, device)

    offsets = jnp.arange(block_len, dtype=jnp.int32)
    own_blocks = lax.dynamic_slice_in_dim(block_of, device * 2, 2, 1)
    row_pos = (own_blocks[:, :, None] * block_len + offsets).reshape(seqs, rows)
    query_pos = jnp.tile(row_pos, (1, heads))[:, None, :]
    flips = jnp.array(
        [core + step + far for core in (0, 1) for step in (0, 2) for far in groups.far_bits],
        jnp.int32,
    )
    key_blocks = block_of.reshape(seqs, ctx, 2)[:, device ^ flips]
    key_pos = (key_blocks[..., None] * block_len + offsets).reshape(seqs, ctx * rows, 1)
    cosine, sine = rope_tables(row_pos.reshape(count), HEAD)
    cosine, sine = jnp.tile(cosine, (1, 2)), jnp.tile(sine, (1, 2))

    qkv_width = query_width + 2 * HEAD
    row = jnp.arange(width)[:, None] % share
    unit = jnp.arange(qkv_width)[None, :]
    same = (row == unit % share).astype(jnp.bfloat16)
    column = (unit.T // share + 2 == jnp.arange(128)[None, :]).astype(jnp.float32)
    w_ffn, w_attn, key_pos, query_pos, cosine, sine, same, column = together(
        w_ffn, w_attn, key_pos, query_pos, cosine, sine, same, column
    )
    w_ffn = lax.all_gather(w_ffn, "ctx", axis=0, tiled=True, axis_index_groups=groups.far)
    w_qkv = groups.spread_near(w_attn[:, :, :qkv_width])
    grads_in = cotangent.reshape(count, width)

    bias = jnp.concatenate([b_query, b_key, b_value]).astype(jnp.float32)[None]
    normed_low, queries, pair = whole_call(
        functools.partial(project_kernel, heads),
        "project",
        (tokens.reshape(count, width), w_qkv, bias, cosine, sine),
        [
            jax.ShapeDtypeStruct((count, width), jnp.bfloat16),
            jax.ShapeDtypeStruct((count, query_width), jnp.bfloat16),
            jax.ShapeDtypeStruct((count, 2 * HEAD), jnp.bfloat16),
        ],
    )
    queries = queries.reshape(seqs, rows, query_width)
    pairs = groups.far_flips(pair)
    w_out_t = groups.flip_near(w_attn[:, :, qkv_width:], device)
    pairs = jnp.stack([pairs, groups.flip(pairs, 2)])
    pairs = jnp.stack([pairs, groups.flip(pairs, 1)]).reshape(ctx, seqs, rows, 2 * HEAD)
    pairs, w_out_t = together(pairs, w_out_t)
    attend = functools.partial(
        attention_call, heads=heads, rows=rows, ctx=ctx, seqs=seqs, width=width
    )
    tall = heads * rows
    tall_kind = "out" if ctx * rows > 1024 else "none"
    out_flat, attention, out_tall, log_total = attend(
        forward_kernel,
        "forward",
        inputs=(queries, pairs, key_pos, query_pos, w_out_t),
        kinds=("flat", "pair", "key", "row", "weight"),
        outs=(
            ("flat", jnp.bfloat16),
            ("model", jnp.bfloat16),
            (tall_kind, jnp.float32),
            ("row", jnp.float32),
        ),
        scratch=[
            ((1, tall), jnp.float32),
            ((1, tall), jnp.float32),
            ((2 * HEAD, tall), jnp.float32),
        ],
    )
    out_flat = out_flat.reshape(count, query_width)
    inputs = tokens.astype(jnp.float32).reshape(count, width)
    hidden = inputs + sum_tp(attention.reshape(count, width))

    grads_near = groups.gather_near(grads_in)
    hidden, *grads_near = together(hidden, *grads_near)
    normed_two, _ = norm_apply(hidden)
    near_two = groups.gather_near(normed_two.astype(jnp.bfloat16))
    token_parts = jnp.concatenate([*near_two, *grads_near], axis=0)
    near_kept, near_sent, mixed_kept, mixed_sent, d_w_ffn = ffn_call(part, token_parts, w_ffn)
    d_w_ffn = lax.psum_scatter(
        d_w_ffn, "ctx", scatter_dimension=0, tiled=True, axis_index_groups=groups.far
    )
    crossed = groups.flip(near_sent, 1)
    near_sent = groups.flip(add(near_kept[count:], crossed[count:]), 2)
    d_own = add(add(near_kept[:count], crossed[:count]), near_sent)
    mixed_sent = groups.flip(mixed_sent, 1)
    d_own, mixed_sent = together(d_own, mixed_sent)
    d_other = lax.ppermute(d_own, "tp", [(0, 1), (1, 0)])
    mixed_kept = add(mixed_kept, mixed_sent)
    d_other, mixed_kept = together(d_other, mixed_kept)
    mixed_own = add(mixed_kept[:count], groups.flip(mixed_kept[count:], 2))

    by_seq = lambda values: values.reshape((seqs, rows) + values.shape[1:])
    d_hidden, d_hidden_low, d_query_low, d_pairs = attend(
        backward_kernel,
        "backward",
        inputs=(
            queries,
            pairs,
            key_pos,
            query_pos,
            out_tall,
            log_total,
            w_out_t,
            by_seq(d_own),
            by_seq(d_other),
            by_seq(hidden),
            cotangent,
            by_seq(cosine),
            by_seq(sine),
        ),
        kinds=(
            ("flat", "pair", "key", "row", tall_kind, "row", "weight")
            + ("model", "model", "model", "model", "table", "table")
        ),
        outs=(
            ("model", jnp.float32),
            ("model", jnp.bfloat16),
            ("flat", jnp.bfloat16),
            ("pair", jnp.bfloat16),
        ),
        scratch=[
            ((tall, 2 * HEAD), jnp.bfloat16),
            ((1, tall), jnp.float32),
            ((2 * HEAD, tall), jnp.float32),
        ],
    )
    d_hidden = d_hidden.reshape(count, width)
    d_hidden_low = d_hidden_low.reshape(count, width)
    d_query_low = d_query_low.reshape(count, query_width)
    d_pairs, mixed_own = together(d_pairs, mixed_own)
    mixed_other = lax.ppermute(mixed_own, "tp", [(0, 1), (1, 0)])
    d_pairs = d_pairs.reshape(2, 2 * groups.high * count, 2 * HEAD)
    crossed = groups.flip(d_pairs[1], 1)
    crossed, d_query_low = together(crossed, d_query_low)
    halves = lambda columns: [jax.ShapeDtypeStruct((ctx // 2, share, columns), jnp.bfloat16)] * 2
    wide_kept, wide_sent = whole_call(
        functools.partial(wide_kernel, share),
        "wide",
        (normed_low, d_query_low, d_hidden_low, out_flat),
        halves(2 * query_width),
        place=device,
    )
    wide_crossed = groups.flip(wide_sent, 1)
    d_pairs = add(d_pairs[0], crossed).reshape(2, groups.high * count, 2 * HEAD)
    d_pairs = add(d_pairs[0], groups.flip(d_pairs[1], 2)).reshape(groups.high, count, 2 * HEAD)
    d_pairs, wide_crossed = together(d_pairs, wide_crossed)

    def near_half(kept, crossed):
        pieces = add(kept, crossed).reshape((groups.high, 2) + kept.shape[1:])
        mine = device // 2 % 2
        sent = lax.dynamic_index_in_dim(pieces, 1 - mine, 1, False)
        return lax.dynamic_index_in_dim(pieces, mine, 1, False), groups.flip(sent, 2)

    wide_kept, wide_beside = near_half(wide_kept, wide_crossed)
    pair_grads = d_pairs[0].astype(jnp.float32)
    for m in range(1, groups.high):
        pair_grads = pair_grads + groups.flip(d_pairs[m], groups.far_bits[m]).astype(jnp.float32)
    pair_grads, wide_beside = together(pair_grads, wide_beside)
    mixed = hidden + mixed_own.astype(jnp.float32) + mixed_other.astype(jnp.float32)
    mixed = mixed.astype(jnp.bfloat16)

    d_weighted_low, narrow_kept, narrow_sent = whole_call(
        functools.partial(finish_kernel, share),
        "finish",
        (
            pair_grads,
            cosine,
            sine,
            normed_low,
            tokens.reshape(count, width),
            w_qkv,
            d_query_low,
            d_own,
            d_other,
            hidden,
            same,
            column,
        ),
        [
            jax.ShapeDtypeStruct((count, width), jnp.bfloat16),
            *halves(256),
        ],
        place=device,
    )
    narrow_kept, narrow_beside = near_half(narrow_kept, groups.flip(narrow_sent, 1))
    narrow = add(narrow_kept, narrow_beside)
    extra = narrow[:, :, 2 * HEAD :]
    other = lax.ppermute(extra, "tp", [(0, 1), (1, 0)])
    first = lax.broadcasted_iota(jnp.int32, extra.shape, 2) == 0
    extra = jnp.where(first, add(extra, other), extra)
    narrow = jnp.concatenate(
        [add(wide_kept, wide_beside), narrow[:, :, : 2 * HEAD], extra], axis=2
    )
    narrow, d_w_ffn, d_weighted_low, mixed = together(narrow, d_w_ffn, d_weighted_low, mixed)
    d_weighted = sum_tp(d_weighted_low)
    _, scale_one = norm_apply(inputs)
    tokens_grad = (d_hidden + norm_back(inputs, scale_one, d_weighted)).astype(jnp.bfloat16)
    d_w_ffn = groups.swap_near(d_w_ffn.reshape(low, share, 3 * part))
    narrow = groups.far_owner(narrow, device)
    d_w_wide, narrow = narrow[:, : 2 * query_width], narrow[:, 2 * query_width :]

    def whole(swapped, index):
        some = swapped[:, :, index * part : (index + 1) * part].transpose(1, 0, 2)
        return some.reshape(share, low * part)[:, :units].astype(jnp.float32)

    g_gate = whole(d_w_ffn, 0) * own_gain_two
    g_up = whole(d_w_ffn, 1) * own_gain_two
    g_down = whole(d_w_ffn, 2).T

    held = -(-qkv_width // share)
    g_bias = narrow[:, 2 * HEAD + 2 : 2 * HEAD + 2 + held].T.reshape(held * share)
    g_pair = narrow[:, : 2 * HEAD] * own_gain_one
    g_two = narrow[:, 2 * HEAD + 1] / own_gain_two[:, 0]
    g_one = narrow[:, 2 * HEAD] / own_gain_one[:, 0]
    return (
        mixed.reshape(tokens.shape),
        tokens_grad.reshape(tokens.shape),
        g_one,
        g_two,
        d_w_wide[:, :query_width] * own_gain_one,
        g_pair[:, :HEAD],
        g_pair[:, HEAD:],
        g_bias[:query_width],
        g_bias[query_width : query_width + HEAD],
        g_bias[query_width + HEAD : query_width + 2 * HEAD],
        d_w_wide[:, query_width:].T,
        g_gate,
        g_up,
        g_down,
    )


def solution(mesh):
    placed = (
        P(None, "ctx", None),
        P(None, "ctx", None),
        P(),
        P("ctx"),
        P("ctx"),
        P("ctx", "tp"),
        P("ctx", "tp"),
        P("ctx", "tp"),
        P("tp"),
        P("tp"),
        P("tp"),
        P("tp", "ctx"),
        P("ctx", "tp"),
        P("ctx", "tp"),
        P("tp", "ctx"),
    )
    return jax.shard_map(
        local,
        mesh=mesh,
        in_specs=placed,
        out_specs=(
            P(None, "ctx", None),
            P(None, "ctx", None),
            P("ctx"),
            P("ctx"),
            P("ctx", "tp"),
            P("ctx", "tp"),
            P("ctx", "tp"),
            P("tp"),
            P("tp"),
            P("tp"),
            P("tp", "ctx"),
            P("ctx", "tp"),
            P("ctx", "tp"),
            P("tp", "ctx"),
        ),
        check_vma=False,
    )
```
